32 devices in a mesh: groups: 2 (over x), blk: 8 (over z, y), heads: 2 (over core).
Axes of the slice: x: 2, y: 2, z: 4, core: 2. Of those that a mesh axis runs over, the one named last changes fastest.
Arguments:
- image_feats: bfloat16 [4096, 8192], P(('groups', 'blk')), parts along dimension 0, may hold values from -6 to 6
- slot_image: int32 [4096], P(('groups', 'blk')), parts along dimension 0, may hold values from -1 to 3, as said below
- key_weight: bfloat16 [8192, 512], P('blk', 'heads'), may hold values from -0.0625 to 0.0625
- value_weight: bfloat16 [8192, 512], P('blk', 'heads'), may hold values from -0.0625 to 0.0625
- key_gain: float32 [128], replicated, may hold values from 0.25 to 1.75
- queries: bfloat16 [512, 4096], P(('groups', 'blk'), 'heads'), parts along dimension 0, may hold values from -60 to 60
- text_image: int32 [512], P('groups'), parts along dimension 0, may hold values from 0 to 3
- text_hidden: bfloat16 [512, 8192], P(('groups', 'heads'), 'blk'), parts along dimension 0, may hold values from -4 to 4
- out_weight: bfloat16 [4096, 8192], P('heads', 'blk'), may hold values from -0.09375 to 0.09375
- attn_gate: float32 [1], replicated, may hold values from 0.4 to 1.2
Outputs:
- mixed: bfloat16 [512, 8192], P(('groups', 'heads'), 'blk'), parts along dimension 0
The draws below stay inside these ranges and needn't reach their ends.
There are 2 independent parts, one for each index of `groups`. The reference program is written for one: setup_inputs(seed, part) draws one part's arguments, and reference() takes and returns one part's arrays. A program takes and returns all parts, laid end to end along the dimension named above; an argument that names none is the same for every part. Nothing has to cross between parts.
Inputs may be any that keep to these rules, and one draw needn't show every extreme that they name: `slot_image`: slots come in tiles of 64; the live slots of a tile come first and carry one image id, -1 marks an empty slot; every image has live slots; the first 256 slots are all live.
All inputs are finite; a program needn't handle non-finite values.
Results may differ from the reference program's by a relative error of at most 0.008.
Values may be sent and summed in bfloat16 or wider, within the bound.
No kernel may reach another device: no remote copies, remote signals or barrier semaphores. Data moves between devices by JAX's collectives and lax.ppermute only.
A program may use at most 128 MiB of HBM per device.

```python
import math
import jax
import jax.numpy as jnp
from jax import lax

D = 8192
DV = 8192
HQ = 32
KVH = 4
HD = 128
IMAGES = 4
TILE = 64
TOK_DEV = 256
IMG = 2048
TEXT = 256


def draw_slot_image(key, part):
    tile_count = IMG // TILE
    per_dev = TOK_DEV // TILE
    devices_count = tile_count // per_dev
    key_a, key_b, key_c, key_d = jax.random.split(jax.random.fold_in(key, 11), 4)
    fill_level = jax.random.randint(key_a, (devices_count,), 0, 8)
    tile_index = jnp.arange(tile_count)
    owner_dev = tile_index // per_dev
    first_tiles = tile_index < IMAGES
    live_tile = jax.random.randint(key_b, (tile_count,), 0, 10) < 3 + fill_level[owner_dev]
    live_tile = live_tile | (owner_dev == 0) | first_tiles
    image_id = jax.random.randint(key_c, (tile_count,), 0, IMAGES)
    image_id = jnp.where(first_tiles, tile_index % IMAGES, image_id)
    token_count = jax.random.randint(key_d, (tile_count,), TILE // 2, TILE + 1)
    token_count = jnp.where(owner_dev == 0, TILE, token_count)
    position = jnp.arange(TILE)
    slot_ids = jnp.where(live_tile[:, None] & (position[None, :] < token_count[:, None]), image_id[:, None], -1)
    return slot_ids.reshape(IMG).astype(jnp.int32)


def draw_queries(key, part):
    base = jax.random.normal(jax.random.fold_in(key, 23), (TEXT, HQ * HD), jnp.float32)
    drawn = jnp.clip(2.0 * base, -12.0, 12.0)
    return drawn.astype(jnp.bfloat16)


def plant(array, own_key, low, largest):
    dims = array.shape
    spot = [jax.random.randint(jax.random.fold_in(own_key, axis), (), 0, dims[axis]) for axis in range(len(dims))]
    array = array.at[tuple(spot)].set(low)
    longest = dims.index(max(dims))
    spot[longest] = (spot[longest] + 1) % dims[longest]
    return array.at[tuple(spot)].set(largest)


def block_scale(own_key, shape, pieces, low, top_value):
    def one(axis_at, parts):
        draws = jax.random.uniform(jax.random.fold_in(jax.random.fold_in(own_key, 6), axis_at), (parts,), jnp.float32, low / len(pieces), top_value / len(pieces))
        return jnp.repeat(jnp.exp(draws), shape[axis_at] // parts).reshape((-1,) + (1,) * (len(shape) - axis_at - 1))

    factor_of = one(*pieces[0])
    for cut in pieces[1:]:
        factor_of = factor_of * one(*cut)
    return factor_of


def bell_draw(rng, shape, deviation, limit, cuts=(), kind=jnp.bfloat16):
    values = jax.random.normal(rng, shape, jnp.float32) * deviation
    if len(cuts) > 0:
        values = block_scale(rng, shape, cuts, -0.22, 0.18) * values
    return jnp.clip(values, min=-limit, max=limit).astype(kind)


def setup_inputs(seed: int = 0, part: int = 0) -> dict:
    arg_keys = jax.random.split(jax.random.key(seed), 11)
    own_keys = jax.random.split(jax.random.fold_in(arg_keys[10], part), 11)
    image_feats = bell_draw(own_keys[0], (IMG, DV), 1.0, 6.0, ((0, 8),))
    slot_image = draw_slot_image(jax.random.fold_in(jax.random.fold_in(arg_keys[10], part), 71), part)
    key_weight = bell_draw(arg_keys[2], (DV, KVH * HD), DV ** -0.5, 0.0625, ((0, 8), (1, 2)))
    value_weight = bell_draw(arg_keys[3], (DV, KVH * HD), DV ** -0.5, 0.0625, ((0, 8), (1, 2)))
    key_gain = jnp.clip(1.0 + 0.15 * jax.random.normal(arg_keys[4], (HD,), jnp.float32), 0.25, 1.75)
    queries = draw_queries(jax.random.fold_in(jax.random.fold_in(arg_keys[10], part), 71), part)
    text_image = plant(jax.random.randint(own_keys[6], (TEXT,), 0, IMAGES), jax.random.fold_in(own_keys[6], 1), 0, IMAGES - 1).astype(jnp.int32)
    text_hidden = bell_draw(own_keys[7], (TEXT, D), 0.5, 4.0, ((0, 2), (1, 8)))
    out_weight = bell_draw(arg_keys[8], (HQ * HD, D), (HQ * HD) ** -0.5, 0.09375, ((0, 2), (1, 8)))
    attn_gate = jnp.clip(jax.random.uniform(arg_keys[9], (1,), jnp.float32, 0.4, 1.2), 0.4, 1.2)
    return dict(image_feats=image_feats, slot_image=slot_image, key_weight=key_weight, value_weight=value_weight, key_gain=key_gain, queries=queries, text_image=text_image, text_hidden=text_hidden, out_weight=out_weight, attn_gate=attn_gate)


def reference(image_feats, slot_image, key_weight, value_weight, key_gain, queries, text_image, text_hidden, out_weight, attn_gate):
    keys_raw = jnp.dot(image_feats, key_weight, preferred_element_type=jnp.float32).reshape(IMG, KVH, HD)
    norm_scale = lax.rsqrt(lax.optimization_barrier(jnp.mean(keys_raw * keys_raw, axis=-1, keepdims=True)) + 1e-05)
    keys = (keys_raw * norm_scale * key_gain).astype(jnp.bfloat16)
    values = jnp.dot(image_feats, value_weight, preferred_element_type=jnp.float32).astype(jnp.bfloat16).reshape(IMG, KVH, HD)
    visible = (slot_image[None, :] >= 0) & (slot_image[None, :] <= text_image[:, None])
    score_scale = 1.0 / math.sqrt(HD)
    per_kv = HQ // KVH

    def one_head(head):
        group_id = head // per_kv
        query_head = lax.dynamic_slice_in_dim(queries, head * HD, HD, 1)
        key_head = lax.dynamic_index_in_dim(keys, group_id, 1, keepdims=False)
        value_head = lax.dynamic_index_in_dim(values, group_id, 1, keepdims=False)
        scores = jnp.dot(query_head, key_head.T, preferred_element_type=jnp.float32) * score_scale
        row_top = lax.optimization_barrier(jnp.max(jnp.where(visible, scores, -1e+30), axis=1, keepdims=True))
        expo = jnp.where(visible, jnp.exp(scores - row_top), 0.0)
        numerator = jnp.dot(expo.astype(jnp.bfloat16), value_head, preferred_element_type=jnp.float32)
        return (numerator / lax.optimization_barrier(jnp.sum(expo, axis=1, keepdims=True))).astype(jnp.bfloat16)
    heads_out = lax.map(one_head, jnp.arange(HQ).astype(jnp.int32))
    attn = jnp.transpose(heads_out, (1, 0, 2)).reshape(TEXT, HQ * HD)
    proj = jnp.dot(attn, out_weight, preferred_element_type=jnp.float32)
    return (text_hidden.astype(jnp.float32) + jnp.tanh(attn_gate[0]) * proj).astype(jnp.bfloat16)
```

```python
import functools
import math

import jax
import jax.numpy as jnp
from jax import lax
from jax.experimental import pallas as pl
from jax.experimental.pallas import tpu as pltpu
from jax.sharding import PartitionSpec as P

HD = 128
F32 = jnp.float32
BF16 = jnp.bfloat16
VMEM_BYTES = 48 * 1024 * 1024
PARAMS = pltpu.CompilerParams(vmem_limit_bytes=VMEM_BYTES)
WHOLE = pl.BlockSpec(memory_space=pltpu.VMEM)


def dot(a, b):
    return jnp.dot(a, b, preferred_element_type=F32)


def dot_nt(a, b):
    return lax.dot_general(a, b, (((1,), (1,)), ((), ())), preferred_element_type=F32)


def shard_kernel(n_w, first, idx_ref, own_m, own_o, par_m, par_o, *refs):
    rows = own_m.shape[0]
    w_m, w_o = refs[0][...], refs[1][...]
    if n_w == 2:
        take_up = idx_ref[3] > 0
        w_m = jnp.where(take_up, w_m, refs[2][...])
        w_o = jnp.where(take_up, w_o, refs[3][...])
    out = refs[-1]
    top = dot(own_m[...], w_m) + dot(own_o[...], w_o)
    low = dot(par_m[...], w_m) + dot(par_o[...], w_o)
    if not first:
        acc = refs[-2]
        top = top + acc[:rows, :]
        low = low + acc[rows:, :]
    out[:rows, :] = top
    out[rows:, :] = low


def shard_dot(idx, image, partner, weights, acc, own_weight):
    rows = image.shape[0]
    half = weights[0].shape[0] // (2 if own_weight else 1)
    cols = weights[0].shape[1]
    first = acc is None
    specs = [
        pl.BlockSpec((rows, half), lambda i, s: (0, 2 * s[0] + s[2])),
        pl.BlockSpec((rows, half), lambda i, s: (0, 2 * s[0] + 1 - s[2])),
        pl.BlockSpec((rows, half), lambda i, s: (0, 2 * s[1] + s[2])),
        pl.BlockSpec((rows, half), lambda i, s: (0, 2 * s[1] + 1 - s[2])),
    ]
    args = [image, image, partner, partner]
    if own_weight:
        specs += [
            pl.BlockSpec((half, cols), lambda i, s: (s[2], 0)),
            pl.BlockSpec((half, cols), lambda i, s: (1 - s[2], 0)),
        ]
        args += [weights[0], weights[0]]
        n_w = 1
    else:
        specs += [pl.BlockSpec((half, cols), lambda i, s: (0, 0))] * len(weights)
        args += list(weights)
        n_w = len(weights) // 2
    aliases = {}
    if not first:
        specs.append(pl.BlockSpec((2 * rows, cols), lambda i, s: (0, 0)))
        args.append(acc)
        aliases = {len(args): 0}
    return pl.pallas_call(
        functools.partial(shard_kernel, n_w, first),
        out_shape=jax.ShapeDtypeStruct((2 * rows, cols), F32),
        grid_spec=pltpu.PrefetchScalarGridSpec(
            num_scalar_prefetch=1,
            grid=(1,),
            in_specs=specs,
            out_specs=pl.BlockSpec((2 * rows, cols), lambda i, s: (0, 0)),
        ),
        input_output_aliases=aliases,
        compiler_params=PARAMS,
        cost_estimate=pl.CostEstimate(
            flops=8 * rows * half * cols, bytes_accessed=8 * rows * half + 4 * half * cols, transcendentals=0
        ),
    )(idx, *args)


def score_kernel(n, heads, q_ref, limit_ref, *refs):
    keys, slots = refs[:n], refs[n : 2 * n]
    expo_ref, total_ref, s_ref = refs[2 * n :]
    rows = limit_ref.shape[0]
    piece = keys[0].shape[0]
    scale = 1.0 / math.sqrt(HD)
    limit = limit_ref[...]
    top = jnp.full((heads * rows, 1), -1e30, F32)
    for i in range(n):
        slot = slots[i][...]
        visible = (slot >= 0.0) & (slot <= limit)
        bias = jnp.where(visible, 0.0, -1e30)
        s = dot_nt(q_ref[...], keys[i][...]) * scale
        s = jnp.where(bias[None] < 0.0, -1e30, s.reshape(heads, rows, piece)).reshape(heads * rows, piece)
        s_ref[:, i * piece : (i + 1) * piece] = s
        top = jnp.maximum(top, jnp.max(s, axis=1, keepdims=True))
    total = jnp.zeros((heads * rows, 1), F32)
    for i in range(n):
        s = s_ref[:, i * piece : (i + 1) * piece]
        e = jnp.where(s > -1e29, jnp.exp(s - top), 0.0)
        total = total + jnp.sum(e, axis=1, keepdims=True)
        expo_ref[:, i * piece : (i + 1) * piece] = e.astype(BF16)
    total_ref[...] = total


def value_kernel(n, heads, expo_ref, total_ref, *refs):
    values, out_ref = refs[:n], refs[n]
    rows = out_ref.shape[0]
    piece = values[0].shape[0]
    acc = jnp.zeros((heads * rows, HD), F32)
    for i in range(n):
        acc = acc + dot(expo_ref[:, i * piece : (i + 1) * piece], values[i][...])
    attn = (acc / total_ref[...]).astype(BF16)
    for j in range(heads):
        out_ref[:, j * HD : (j + 1) * HD] = attn[j * rows : (j + 1) * rows, :]


def proj_kernel(n, idx_ref, *refs):
    mine, other = refs[:n], refs[n : 2 * n]
    w_mine, w_other, keep_ref, send_ref, a_ref, p_ref = refs[2 * n :]
    rows, width = mine[0].shape
    for d in range(n):
        a_ref[d * rows : (d + 1) * rows, :width] = mine[d][...]
        a_ref[d * rows : (d + 1) * rows, width:] = other[d][...]
    p_ref[...] = dot(a_ref[:, :width], w_mine[...]) + dot(a_ref[:, width:], w_other[...])
    for k in range(n // 2):
        at_keep = pl.multiple_of(idx_ref[1 + k] * rows, rows)
        at_send = pl.multiple_of(idx_ref[1 + n // 2 + k] * rows, rows)
        keep_ref[k * rows : (k + 1) * rows, :] = p_ref[pl.ds(at_keep, rows), :]
        send_ref[k * rows : (k + 1) * rows, :] = p_ref[pl.ds(at_send, rows), :].astype(BF16)


def body(
    image_feats,
    slot_image,
    key_weight,
    value_weight,
    key_gain,
    queries,
    text_image,
    text_hidden,
    out_weight,
    attn_gate,
):
    groups, nblk, cores = (lax.axis_size(a) for a in ("groups", "blk", "heads"))
    lines = nblk // 2
    tok = image_feats.shape[0]
    depth = key_weight.shape[0]
    kv_cols = key_weight.shape[1]
    mine_cols = kv_cols // 2
    text_rows = queries.shape[0]
    q_half = queries.shape[1] // 2
    per_kv = q_half // mine_cols
    grp, blk, core = (lax.axis_index(a) for a in ("groups", "blk", "heads"))
    par = grp % 2
    y = blk % 2
    line = blk // 2

    swap_y = [(b, b ^ 1) for b in range(nblk)]
    swap_core = [(c, c ^ 1) for c in range(cores)]

    def shift(array, d):
        return lax.ppermute(array, "blk", [(b, b + 2 * d) for b in range(nblk) if 0 <= b + 2 * d < nblk])

    def turn(array, d):
        return lax.ppermute(array, "blk", [(b, (b - 2 * d) % nblk) for b in range(nblk)])

    def swap_x(array, ok):
        pairs = [(g * nblk + b, (g ^ 1) * nblk + b) for g in range(groups) for b in range(nblk) if ok(b // 2)]
        return lax.ppermute(array, ("groups", "blk"), pairs)

    def take_y(array, size, which):
        return lax.dynamic_slice_in_dim(array, which * size, size, 1)

    half_lines = lines // 2
    sends = [
        lax.dynamic_slice_in_dim(image_feats, (2 * (core * half_lines + l) + 1 - y) * depth, depth, 1)
        for l in range(half_lines)
    ]
    got = [lax.ppermute(s, "blk", swap_y) for s in sends]
    got_other = [lax.ppermute(s, "heads", swap_core) for s in got]
    got, got_other = jnp.concatenate(got, 1), jnp.concatenate(got_other, 1)
    low_core = core == 0
    partner = jnp.concatenate(
        [jnp.where(low_core, got, got_other), jnp.where(low_core, got_other, got)], 1
    )

    def project(weight):
        half = depth // 2
        up = dn = lax.dynamic_slice_in_dim(weight, par * half, half, 0)
        zero = jnp.int32(0)
        acc = shard_dot(
            jnp.stack([blk, line, par, zero]), image_feats, partner, [weight], None, True
        )
        for s in range(1, lines):
            up, dn = shift(up, 1), shift(dn, -1)
            up_x = swap_x(up, lambda l: l >= s)
            dn_x = swap_x(dn, lambda l: l + s < lines)
            low, high = jnp.maximum(line - s, 0), jnp.minimum(line + s, lines - 1)
            if 2 * s >= lines:
                is_up = line >= s
                at = jnp.where(is_up, low, high)
                acc = shard_dot(
                    jnp.stack([2 * at + y, at, par, is_up.astype(jnp.int32)]),
                    image_feats, partner, [up, up_x, dn, dn_x], acc, False,
                )
            else:
                acc = shard_dot(
                    jnp.stack([2 * low + y, low, par, zero]), image_feats, partner, [up, up_x], acc, False
                )
                acc = shard_dot(
                    jnp.stack([2 * high + y, high, par, zero]), image_feats, partner, [dn, dn_x], acc, False
                )
        keep = take_y(acc, mine_cols, y)
        send = take_y(acc, mine_cols, 1 - y)
        return keep, jnp.concatenate([send[tok:], send[:tok]], 0)

    keep, send = project(key_weight)
    raw = (keep + lax.ppermute(send, "blk", swap_y)).reshape(2 * tok, mine_cols // HD, HD)
    norm_scale = lax.rsqrt(jnp.mean(raw * raw, axis=-1, keepdims=True) + 1e-05)
    keys = (raw * norm_scale * key_gain).astype(BF16).reshape(2 * tok, mine_cols)

    slots = slot_image.astype(BF16)
    slots = jnp.concatenate([slots, lax.ppermute(slots, "blk", swap_y)]).reshape(2 * tok // HD, HD)
    pad = -slots.shape[0] % 16
    slots = jnp.pad(slots, ((0, pad), (0, 0)))
    packed = jnp.concatenate([keys, slots], 0)
    key_pieces, slot_pieces = [], []
    for d in range(lines):
        piece = packed if d == 0 else turn(packed, d)
        key_pieces.append(piece[: 2 * tok])
        slot_pieces.append(piece[2 * tok : 2 * tok + 2 * tok // HD].astype(F32).reshape(1, 2 * tok))

    q_mine = take_y(queries, q_half, y)
    q_got = lax.ppermute(take_y(queries, q_half, 1 - y), "blk", swap_y)
    is_low = y == 0
    q_rows = jnp.concatenate([jnp.where(is_low, q_mine, q_got), jnp.where(is_low, q_got, q_mine)], 0)
    rows = 2 * text_rows
    q_all = q_rows.reshape(rows, per_kv, HD).transpose(1, 0, 2).reshape(per_kv * rows, HD)
    limit = lax.dynamic_slice_in_dim(text_image, line * rows, rows, 0).astype(F32).reshape(rows, 1)

    tokens = 2 * tok * lines
    expo, total = pl.pallas_call(
        functools.partial(score_kernel, lines, per_kv),
        out_shape=(
            jax.ShapeDtypeStruct((per_kv * rows, tokens), BF16),
            jax.ShapeDtypeStruct((per_kv * rows, 1), F32),
        ),
        in_specs=[WHOLE] * (2 + 2 * lines),
        out_specs=(WHOLE, WHOLE),
        scratch_shapes=[pltpu.VMEM((per_kv * rows, tokens), F32)],
        compiler_params=PARAMS,
    )(q_all, limit, *key_pieces, *slot_pieces)

    keep, send = project(value_weight)
    values = (keep + lax.ppermute(send.astype(BF16), "blk", swap_y).astype(F32)).astype(BF16)
    value_pieces = [values if d == 0 else turn(values, d) for d in range(lines)]

    attn = pl.pallas_call(
        functools.partial(value_kernel, lines, per_kv),
        out_shape=jax.ShapeDtypeStruct((rows, q_half), BF16),
        in_specs=[WHOLE] * (2 + lines),
        out_specs=WHOLE,
        compiler_params=PARAMS,
    )(expo, total, *value_pieces)

    mine = [attn if d == 0 else turn(attn, d) for d in range(lines)]
    other = [lax.ppermute(m, "blk", swap_y) for m in mine]

    out_rows = lines * rows
    out_cols = out_weight.shape[1]
    keep_at = [(core * half_lines + k - line) % lines for k in range(half_lines)]
    send_at = [((1 - core) * half_lines + k - line) % lines for k in range(half_lines)]
    whole2 = lambda shape: pl.BlockSpec(shape, lambda i, s: (0, 0))
    keep, send = pl.pallas_call(
        functools.partial(proj_kernel, lines),
        out_shape=(
            jax.ShapeDtypeStruct((out_rows // 2, out_cols), F32),
            jax.ShapeDtypeStruct((out_rows // 2, out_cols), BF16),
        ),
        grid_spec=pltpu.PrefetchScalarGridSpec(
            num_scalar_prefetch=1,
            grid=(1,),
            in_specs=[whole2((rows, q_half))] * (2 * lines)
            + [
                pl.BlockSpec((q_half, out_cols), lambda i, s: (s[0], 0)),
                pl.BlockSpec((q_half, out_cols), lambda i, s: (1 - s[0], 0)),
            ],
            out_specs=(whole2((out_rows // 2, out_cols)), whole2((out_rows // 2, out_cols))),
            scratch_shapes=[
                pltpu.VMEM((out_rows, 2 * q_half), BF16),
                pltpu.VMEM((out_rows, out_cols), F32),
            ],
        ),
        compiler_params=PARAMS,
    )(jnp.stack([y] + keep_at + send_at), *mine, *other, out_weight, out_weight)
    head_total = keep + lax.ppermute(send, "heads", swap_core).astype(F32)
    return (text_hidden.astype(F32) + jnp.tanh(attn_gate[0]) * head_total).astype(BF16)


def solution(mesh):
    placed = (
        P(("groups", "blk"), None),
        P(("groups", "blk")),
        P("blk", "heads"),
        P("blk", "heads"),
        P(),
        P(("groups", "blk"), "heads"),
        P("groups"),
        P(("groups", "heads"), "blk"),
        P("heads", "blk"),
        P(),
    )
    return jax.shard_map(
        body, mesh=mesh, in_specs=placed, out_specs=P(("groups", "heads"), "blk"), check_vma=False
    )
```

```python
import functools
import math

import jax
import jax.numpy as jnp
from jax import lax
from jax.experimental import pallas as pl
from jax.experimental.pallas import tpu as pltpu
from jax.sharding import PartitionSpec as P

HD = 128
F32 = jnp.float32
BF16 = jnp.bfloat16
VMEM_BYTES = 20 * 1024 * 1024
PARAMS = pltpu.CompilerParams(vmem_limit_bytes=VMEM_BYTES)
BIG = pltpu.CompilerParams(vmem_limit_bytes=52 * 1024 * 1024)
WHOLE = pl.BlockSpec(memory_space=pltpu.VMEM)
FREE = pl.BlockSpec(memory_space=pltpu.HBM)


def dot(a, b):
    return jnp.dot(a, b, preferred_element_type=F32)


def dot_nt(a, b):
    return lax.dot_general(a, b, (((1,), (1,)), ((), ())), preferred_element_type=F32)


def share_kernel(idx_ref, image, key_weight, value_weight, to_y, to_x, to_both, own, sems):
    par, core, y = idx_ref[0], idx_ref[1], idx_ref[2]
    half = own.shape[0] // 2
    half_lines = to_y.shape[1] // half
    copies = []
    at_w = pl.multiple_of(par * half, half)
    copies.append((key_weight.at[pl.ds(at_w, half), :], own.at[pl.ds(0, half), :]))
    copies.append((value_weight.at[pl.ds(at_w, half), :], own.at[pl.ds(half, half), :]))
    for out, to_par, to_y_at in ((to_x, 1 - par, y), (to_y, par, 1 - y), (to_both, 1 - par, 1 - y)):
        for l in range(half_lines):
            at = pl.multiple_of(((2 * (core * half_lines + l) + to_y_at) * 2 + to_par) * half, half)
            copies.append((image.at[:, pl.ds(at, half)], out.at[:, pl.ds(l * half, half)]))
    copies = [pltpu.make_async_copy(src, dst, sems.at[i]) for i, (src, dst) in enumerate(copies)]
    for c in copies:
        c.start()
    for c in copies:
        c.wait()


def project_kernel(sources, extra, idx_ref, slots, image, *refs):
    par, core, y, inner = idx_ref[0], idx_ref[1], idx_ref[2], idx_ref[3]
    got, refs = refs[:6], refs[6:]
    weights, outs, (x_ref, w_ref, acc_ref, sems) = refs[:-8], refs[-8:-4], refs[-4:]
    rows = image.shape[0]
    half = w_ref.shape[1]
    half_lines = got[0].shape[1] // half

    def copy(src, dst, k, i):
        return pltpu.make_async_copy(src, dst, sems.at[k, i])

    waits = []
    for k, (in_src, out_src) in enumerate(sources):
        line = idx_ref[4 + k]
        own_at = pl.multiple_of(((2 * line + y) * 2 + par) * half, half)
        here = line // half_lines == core
        got_at = pl.multiple_of(lax.rem(line, half_lines) * half, half)
        own = copy(image.at[:, pl.ds(own_at, half)], x_ref.at[k, pl.ds(0, rows), :], k, 0)
        own.start()

        def from_core(which, k=k, got_at=got_at):
            return [
                copy(
                    got[2 * i + which].at[:, pl.ds(got_at, half)],
                    x_ref.at[k, pl.ds((i + 1) * rows, rows), :],
                    k,
                    1 + i,
                )
                for i in range(3)
            ]

        def from_weight(src, k=k):
            return copy(weights[src[0]].at[pl.ds(src[1], half), :], w_ref.at[k], k, 4)

        mine = from_core(0)
        weight = from_weight(in_src)

        @pl.when(here)
        def _(mine=mine):
            for c in mine:
                c.start()

        @pl.when(jnp.logical_not(here))
        def _(from_core=from_core):
            for c in from_core(1):
                c.start()

        if in_src == out_src:
            weight.start()
        else:

            @pl.when(inner > 0)
            def _(weight=weight):
                weight.start()

            @pl.when(inner <= 0)
            def _(from_weight=from_weight, out_src=out_src):
                from_weight(out_src).start()

        waits.append([own] + mine + [weight])
    for k in range(len(sources)):
        for c in waits[k]:
            c.wait()
        part = dot(x_ref[k], w_ref[k])
        if k == 0:
            acc_ref[...] = part
        else:
            acc_ref[...] += part
    keep, to_y, to_x, to_both = outs
    cols = keep.shape[1]
    mine = pl.ds(pl.multiple_of(y * cols, cols), cols)
    other = pl.ds(pl.multiple_of((1 - y) * cols, cols), cols)
    kind = to_y.dtype
    keep[...] = acc_ref[: 2 * rows, mine]
    to_y[:rows, :] = acc_ref[rows : 2 * rows, other].astype(kind)
    to_y[rows : 2 * rows, :] = acc_ref[:rows, other].astype(kind)
    to_x[...] = acc_ref[2 * rows :, mine].astype(kind)
    to_both[:rows, :] = acc_ref[3 * rows :, other].astype(kind)
    to_both[rows:, :] = acc_ref[2 * rows : 3 * rows, other].astype(kind)
    if extra:
        n = slots.shape[0]
        to_y[2 * rows : 2 * rows + n, :HD] = slots[...]
        to_y[2 * rows + n :, :] = jnp.zeros((extra - n, cols), kind)
        if cols > HD:
            to_y[2 * rows : 2 * rows + n, HD:] = jnp.zeros((n, cols - HD), kind)


def key_kernel(keep, got_y, got_x, got_both, gain, slots, out):
    rows = keep.shape[0]
    n = slots.shape[0]
    raw = (keep[...] + got_y[:rows, :]) + (got_x[...] + got_both[...])
    for c in range(0, raw.shape[1], HD):
        part = raw[:, c : c + HD]
        scale = lax.rsqrt(jnp.mean(part * part, axis=-1, keepdims=True) + 1e-05)
        out[:rows, c : c + HD] = (part * scale * gain[...]).astype(BF16)
    pad = jnp.zeros((out.shape[0] - rows - 2 * n, HD), F32)
    out[rows:, :HD] = jnp.concatenate([slots[...], got_y[rows : rows + n, :HD], pad], 0).astype(BF16)


def score_kernel(n, heads, q_ref, limit_ref, *refs):
    pieces = refs[:n]
    expo_ref, total_ref, s_ref = refs[n:]
    rows = limit_ref.shape[0]
    piece = s_ref.shape[1] // n
    scale = 1.0 / math.sqrt(HD)
    limit = limit_ref[...]
    top = jnp.full((heads * rows, 1), -1e30, F32)
    for i in range(n):
        slots = pieces[i][piece : piece + 16, :].astype(F32)
        seen = []
        for c in range(piece // HD):
            slot = slots[c : c + 1, :]
            seen.append(jnp.where((slot >= 0.0) & (slot <= limit), 1.0, 0.0))
        seen = jnp.concatenate(seen, 1)
        s = dot_nt(q_ref[...], pieces[i][:piece, :]) * scale
        s = jnp.where(seen[None] > 0.5, s.reshape(heads, rows, piece), -1e30).reshape(heads * rows, piece)
        s_ref[:, i * piece : (i + 1) * piece] = s
        top = jnp.maximum(top, jnp.max(s, axis=1, keepdims=True))
    total = jnp.zeros((heads * rows, 1), F32)
    for i in range(n):
        s = s_ref[:, i * piece : (i + 1) * piece]
        e = jnp.where(s > -1e29, jnp.exp(s - top), 0.0)
        total = total + jnp.sum(e, axis=1, keepdims=True)
        expo_ref[:, i * piece : (i + 1) * piece] = e.astype(BF16)
    total_ref[...] = total


def value_kernel(n, heads, expo_ref, total_ref, *refs):
    values, out_ref = refs[:n], refs[n]
    rows = out_ref.shape[0]
    piece = values[0].shape[0]
    acc = jnp.zeros((heads * rows, HD), F32)
    for i in range(n):
        acc = acc + dot(expo_ref[:, i * piece : (i + 1) * piece], values[i][...])
    attn = (acc / total_ref[...]).astype(BF16)
    for j in range(heads):
        out_ref[:, j * HD : (j + 1) * HD] = attn[j * rows : (j + 1) * rows, :]


def proj_kernel(n, idx_ref, *refs):
    pieces = refs[:n]
    w_ref, keep_ref, send_ref, a_ref, p_ref = refs[n:]
    rows, width = pieces[0].shape

    @pl.when(pl.program_id(0) == 0)
    def _():
        for k in range(n):
            at_row = pl.multiple_of(idx_ref[1 + 2 * k] * rows, rows)
            at_col = pl.multiple_of(idx_ref[2 + 2 * k] * width, width)
            a_ref[pl.ds(at_row, rows), pl.ds(at_col, width)] = pieces[k][...]

    p_ref[...] = dot(a_ref[...], w_ref[...])
    part = keep_ref.shape[0]
    core = idx_ref[0]
    keep_ref[...] = p_ref[pl.ds(pl.multiple_of(core * part, part), part), :]
    send_ref[...] = p_ref[pl.ds(pl.multiple_of((1 - core) * part, part), part), :].astype(BF16)


def body(
    image_feats,
    slot_image,
    key_weight,
    value_weight,
    key_gain,
    queries,
    text_image,
    text_hidden,
    out_weight,
    attn_gate,
):
    groups, nblk, cores = (lax.axis_size(a) for a in ("groups", "blk", "heads"))
    lines = nblk // 2
    tok = image_feats.shape[0]
    depth = key_weight.shape[0]
    kv_cols = key_weight.shape[1]
    mine_cols = kv_cols // 2
    text_rows = queries.shape[0]
    q_half = queries.shape[1] // 2
    per_kv = q_half // mine_cols
    grp, blk, core = (lax.axis_index(a) for a in ("groups", "blk", "heads"))
    par = grp % 2
    y = blk % 2
    line = blk // 2

    swap_y = [(b, b ^ 1) for b in range(nblk)]
    swap_core = [(c, c ^ 1) for c in range(cores)]
    half = depth // 2
    fast = lines == 4 and cores == 2 and kv_cols == 2 * HD

    def along(name, array, d, ok=lambda l: True):
        with jax.named_scope(f"{name}_z{d}"):
            return lax.ppermute(array, "blk", [(b, b ^ (2 * d)) for b in range(nblk) if ok(b // 2)])

    def over_y(name, array):
        with jax.named_scope(name + "_y"):
            return lax.ppermute(array, "blk", swap_y)

    def over_core(name, array):
        with jax.named_scope(name + "_core"):
            return lax.ppermute(array, "heads", swap_core)

    def over_x(name, array):
        with jax.named_scope(name + "_x"):
            return lax.ppermute(array, "groups", [(g, g ^ 1) for g in range(groups)])

    def over_both(name, array):
        pairs = [(g * nblk + b, (g ^ 1) * nblk + (b ^ 1)) for g in range(groups) for b in range(nblk)]
        with jax.named_scope(name + "_xy"):
            return lax.ppermute(array, ("groups", "blk"), pairs)

    def hold(*arrays):
        return lax.optimization_barrier(arrays)

    def take_y(array, size, which):
        return lax.dynamic_slice_in_dim(array, which * size, size, 1)

    def middle(l):
        return l in (1, 2)

    half_lines = lines // 2

    def share(to_x, to_y):
        return jnp.concatenate(
            [
                lax.dynamic_slice_in_dim(
                    image_feats, ((2 * (core * half_lines + l) + to_y) * 2 + to_x) * half, half, 1
                )
                for l in range(half_lines)
            ],
            1,
        )

    half_lines = lines // 2
    scalars = pl.BlockSpec(memory_space=pltpu.SMEM)
    share = jax.ShapeDtypeStruct((tok, half_lines * half), BF16)
    share_y, share_x, share_both, own = pl.pallas_call(
        share_kernel,
        out_shape=(share, share, share, jax.ShapeDtypeStruct((2 * half, kv_cols), BF16)),
        in_specs=[scalars, FREE, FREE, FREE],
        out_specs=(WHOLE,) * 4,
        scratch_shapes=[pltpu.SemaphoreType.DMA((2 + 3 * half_lines,))],
        compiler_params=pltpu.CompilerParams(vmem_limit_bytes=56 * 1024 * 1024),
    )(jnp.stack([par, core, y]), image_feats, key_weight, value_weight)
    if fast:
        z1, zm = along("w", own, 1), along("w", own, 3, middle)
        img_y, img_x = over_y("image", share_y), over_x("image", share_x)
        z1, zm, img_y, img_x, share_both = hold(z1, zm, img_y, img_x, share_both)
        fb, fa = along("w_across", z1, 3, middle), along("w_out", zm, 1, middle)
        img_both = over_both("image", share_both)
        core_y, core_x = over_core("image", img_y), over_core("image", img_x)
        fb, fa, img_both, core_y, core_x = hold(fb, fa, img_both, core_y, core_x)
        core_both = over_core("image", img_both)
        last_k, last_v = along("wk_end", fb[:half], 1, middle), along("wv_end", fb[half:], 1, middle)
        shared = [z1, fb, fa, zm]
        key_refs, value_refs = [own] + shared + [last_k], [own] + shared + [last_v]
        pairs = lambda at: (((0, at), (0, at)), ((1, at), (1, at)), ((2, at), (3, at)), ((4, at), (5, 0)))
        key_from, value_from = pairs(0), pairs(half)
    else:
        img_y, img_x, img_both = over_y("image", share_y), over_x("image", share_x), over_both("image", share_both)
        core_y, core_x, core_both = (over_core("image", i) for i in (img_y, img_x, img_both))
        shards = [own] + [along("w", own, d) for d in range(1, lines)]
        key_refs = value_refs = shards
        key_from = tuple(((d, 0), (d, 0)) for d in range(lines))
        value_from = tuple(((d, half), (d, half)) for d in range(lines))
    pieces = [img_y, core_y, img_x, core_x, img_both, core_both]
    slots = slot_image.astype(F32).reshape(tok // HD, HD)
    extra = 8 * (-(-(tok // HD) // 8))

    def project(weights, sources, extra, kind):
        idx = [par, core, y, ((line == 1) | (line == 2)).astype(jnp.int32)] + [line ^ d for d in range(lines)]
        out = lambda rows, dtype: jax.ShapeDtypeStruct((rows, mine_cols), dtype)
        macs = 4 * tok * half * kv_cols * lines
        return pl.pallas_call(
            functools.partial(project_kernel, sources, extra),
            out_shape=(out(2 * tok, F32), out(2 * tok + extra, kind), out(2 * tok, kind), out(2 * tok, kind)),
            in_specs=[scalars, WHOLE] + [FREE] * (7 + len(weights)),
            out_specs=(WHOLE,) * 4,
            scratch_shapes=[
                pltpu.VMEM((lines, 4 * tok, half), BF16),
                pltpu.VMEM((lines, half, kv_cols), BF16),
                pltpu.VMEM((4 * tok, kv_cols), F32),
                pltpu.SemaphoreType.DMA((lines, 5)),
            ],
            compiler_params=BIG,
            cost_estimate=pl.CostEstimate(flops=2 * macs, bytes_accessed=macs // 64, transcendentals=0),
        )(jnp.stack(idx), slots, image_feats, *pieces, *weights)

    keep, to_y, to_x, to_both = project(key_refs, key_from, extra, F32)
    key_parts = [over_y("key", to_y), over_x("key", to_x), over_both("key", to_both)]
    slot_rows = 2 * tok // HD
    packed = pl.pallas_call(
        key_kernel,
        out_shape=jax.ShapeDtypeStruct((2 * tok + slot_rows + (-slot_rows % 16), mine_cols), BF16),
        in_specs=[WHOLE] * 6,
        out_specs=WHOLE,
        compiler_params=PARAMS,
    )(keep, *key_parts, key_gain.reshape(1, HD), slots)

    rows = 2 * text_rows
    if fast:
        def to_head(name, tile):
            pairs = [
                ((2 * l + yy) * cores + c, (2 * (2 * c + yy) + l % 2) * cores + l // 2)
                for l in range(lines)
                for yy in range(2)
                for c in range(cores)
            ]
            with jax.named_scope(name + "_head"):
                tile = lax.ppermute(tile, ("blk", "heads"), pairs)
            there = over_y(name + "_tile", tile)
            return [tile, there, over_core(name + "_tile", tile), over_core(name + "_tile", there)]

        def query_round(r):
            pairs = [
                ((2 * l + yy) * cores + c, (2 * (2 * c + (r ^ yy)) + l % 2) * cores + l // 2)
                for l in range(lines)
                for yy in range(2)
                for c in range(cores)
            ]
            with jax.named_scope("q_head"):
                return lax.ppermute(take_y(queries, q_half, y ^ r), ("blk", "heads"), pairs)

        q_0, q_1 = query_round(0), query_round(1)
        is_low = line % 2 == 0
        row_at = 2 * core + y
    else:

        def to_head(name, tile):
            return [tile if d == 0 else along(name, tile, d) for d in range(lines)]

        q_0, q_1 = take_y(queries, q_half, y), over_y("q", take_y(queries, q_half, 1 - y))
        is_low = y == 0
        row_at = line
    q_rows = jnp.concatenate([jnp.where(is_low, q_0, q_1), jnp.where(is_low, q_1, q_0)], 0)
    q_all = q_rows.reshape(rows, per_kv, HD).transpose(1, 0, 2).reshape(per_kv * rows, HD)
    limit = lax.dynamic_slice_in_dim(text_image, row_at * rows, rows, 0).astype(F32).reshape(rows, 1)

    key_pieces = to_head("key", packed)

    tokens = 2 * tok * lines
    expo, total = pl.pallas_call(
        functools.partial(score_kernel, lines, per_kv),
        out_shape=(
            jax.ShapeDtypeStruct((per_kv * rows, tokens), BF16),
            jax.ShapeDtypeStruct((per_kv * rows, 1), F32),
        ),
        in_specs=[WHOLE] * (2 + lines),
        out_specs=(WHOLE, WHOLE),
        scratch_shapes=[pltpu.VMEM((per_kv * rows, tokens), F32)],
        compiler_params=PARAMS,
    )(q_all, limit, *key_pieces)

    keep, to_y, to_x, to_both = project(value_refs, value_from, 0, BF16)
    value_parts = [over_y("value", to_y), over_x("value", to_x), over_both("value", to_both)]
    value_y, value_x, value_both = (part.astype(F32) for part in value_parts)
    values = ((keep + value_y) + (value_x + value_both)).astype(BF16)
    value_pieces = to_head("value", values)

    attn = pl.pallas_call(
        functools.partial(value_kernel, lines, per_kv),
        out_shape=jax.ShapeDtypeStruct((rows, q_half), BF16),
        in_specs=[WHOLE] * (2 + lines),
        out_specs=WHOLE,
        compiler_params=PARAMS,
    )(expo, total, *value_pieces)

    where = []
    if fast:
        mine = []
        for k in range(lines):
            pairs = [
                ((2 * l + yy) * cores + c, (2 * ((2 * (l % 2) + c) ^ k) + yy) * cores + l // 2)
                for l in range(lines)
                for yy in range(2)
                for c in range(cores)
            ]
            with jax.named_scope(f"attn_out{k}"):
                mine.append(lax.ppermute(attn, ("blk", "heads"), pairs))
            where.append((2 * ((line ^ k) % 2), (line ^ k) // 2))
        where = [(at + y, col) for at, col in where] + [(at + 1 - y, col) for at, col in where]
    else:
        mine = [attn if d == 0 else along("attn", attn, d) for d in range(lines)]
        where = [(line ^ d, y) for d in range(lines)] + [(line ^ d, 1 - y) for d in range(lines)]
    other = [over_y(f"attn{d}", m) for d, m in enumerate(mine)]

    out_rows = lines * rows
    out_cols = out_weight.shape[1]
    tile = out_cols // max(1, out_cols // 256)
    out_spec = pl.BlockSpec((out_rows // 2, tile), lambda i, s: (0, i))
    keep, send = pl.pallas_call(
        functools.partial(proj_kernel, 2 * lines),
        out_shape=(
            jax.ShapeDtypeStruct((out_rows // 2, out_cols), F32),
            jax.ShapeDtypeStruct((out_rows // 2, out_cols), BF16),
        ),
        grid_spec=pltpu.PrefetchScalarGridSpec(
            num_scalar_prefetch=1,
            grid=(out_cols // tile,),
            in_specs=[pl.BlockSpec((rows, q_half), lambda i, s: (0, 0))] * (2 * lines)
            + [pl.BlockSpec((2 * q_half, tile), lambda i, s: (0, i))],
            out_specs=(out_spec, out_spec),
            scratch_shapes=[pltpu.VMEM((out_rows, 2 * q_half), BF16), pltpu.VMEM((out_rows, tile), F32)],
        ),
        compiler_params=BIG,
    )(jnp.stack([core] + [i for pair in where for i in pair]), *mine, *other, out_weight)
    head_total = keep + over_core("proj", send).astype(F32)
    return (text_hidden.astype(F32) + jnp.tanh(attn_gate[0]) * head_total).astype(BF16)


def solution(mesh):
    placed = (
        P(("groups", "blk"), None),
        P(("groups", "blk")),
        P("blk", "heads"),
        P("blk", "heads"),
        P(),
        P(("groups", "blk"), "heads"),
        P("groups"),
        P(("groups", "heads"), "blk"),
        P("heads", "blk"),
        P(),
    )
    return jax.shard_map(
        body, mesh=mesh, in_specs=placed, out_specs=P(("groups", "heads"), "blk"), check_vma=False
    )
```

```python
import functools
import math

import jax
import jax.numpy as jnp
from jax import lax
from jax.experimental import pallas as pl
from jax.experimental.pallas import tpu as pltpu
from jax.sharding import PartitionSpec as P

HD = 128
F32 = jnp.float32
BF16 = jnp.bfloat16
VMEM_BYTES = 20 * 1024 * 1024
PARAMS = pltpu.CompilerParams(vmem_limit_bytes=VMEM_BYTES)
BIG = pltpu.CompilerParams(vmem_limit_bytes=52 * 1024 * 1024)
WHOLE = pl.BlockSpec(memory_space=pltpu.VMEM)
FREE = pl.BlockSpec(memory_space=pltpu.HBM)


def dot(a, b):
    return jnp.dot(a, b, preferred_element_type=F32)


def dot_nt(a, b):
    return lax.dot_general(a, b, (((1,), (1,)), ((), ())), preferred_element_type=F32)


def share_kernel(flips, half_lines, idx_ref, image, *refs):
    par, core, y = idx_ref[0], idx_ref[1], idx_ref[2]
    n = len(flips)
    with_weights = len(refs) > n + 1
    weights, outs, sems = refs[: 2 * with_weights], refs[2 * with_weights : -1], refs[-1]
    copies = []
    if with_weights:
        own = outs[n]
        half = own.shape[0] // 2
        at_w = pl.multiple_of(par * half, half)
        for i in range(2):
            copies.append((weights[i].at[pl.ds(at_w, half), :], own.at[pl.ds(i * half, half), :]))
    for (flip_x, flip_y), out in zip(flips, outs):
        half = out.shape[1] // half_lines
        to_par = 1 - par if flip_x else par
        to_y = 1 - y if flip_y else y
        for l in range(half_lines):
            at = pl.multiple_of(((2 * (core * half_lines + l) + to_y) * 2 + to_par) * half, half)
            copies.append((image.at[:, pl.ds(at, half)], out.at[:, pl.ds(l * half, half)]))
    copies = [pltpu.make_async_copy(src, dst, sems.at[i]) for i, (src, dst) in enumerate(copies)]
    for c in copies:
        c.start()
    for c in copies:
        c.wait()


def load_shards(first, sources, idx_ref, image, got, weights, x_ref, w_ref, sems):
    par, core, y, inner = idx_ref[0], idx_ref[1], idx_ref[2], idx_ref[3]
    rows = image.shape[0]
    half = x_ref.shape[2]
    half_lines = got[0].shape[1] // half
    cols = weights[0].shape[1]

    def copy(src, dst, k, i):
        return pltpu.make_async_copy(src, dst, sems.at[k, i])

    waits = []
    for k, projections in enumerate(sources):
        line = idx_ref[4 + first + k]
        own_at = pl.multiple_of(((2 * line + y) * 2 + par) * half, half)
        here = line // half_lines == core
        got_at = pl.multiple_of(lax.rem(line, half_lines) * half, half)
        own = copy(image.at[:, pl.ds(own_at, half)], x_ref.at[k, pl.ds(0, rows), :], k, 0)
        own.start()

        def from_core(which, k=k, got_at=got_at):
            return [
                copy(
                    got[2 * i + which].at[:, pl.ds(got_at, half)],
                    x_ref.at[k, pl.ds((i + 1) * rows, rows), :],
                    k,
                    1 + i,
                )
                for i in range(3)
            ]

        mine = from_core(0)

        @pl.when(here)
        def _(mine=mine):
            for c in mine:
                c.start()

        @pl.when(jnp.logical_not(here))
        def _(from_core=from_core):
            for c in from_core(1):
                c.start()

        waits.append([own] + mine)
        for p, (in_src, out_src) in enumerate(projections):

            def from_weight(src, k=k, p=p):
                return copy(
                    weights[src[0]].at[pl.ds(src[1], half), :], w_ref.at[k, :, pl.ds(p * cols, cols)], k, 4 + p
                )

            weight = from_weight(in_src)
            if in_src == out_src:
                weight.start()
            else:

                @pl.when(inner > 0)
                def _(weight=weight):
                    weight.start()

                @pl.when(inner <= 0)
                def _(from_weight=from_weight, out_src=out_src):
                    from_weight(out_src).start()

            waits[-1].append(weight)
    return waits


def partial_kernel(sources, idx_ref, image, *refs):
    got, weights = refs[:6], refs[6:-5]
    outs, (x_ref, w_ref, sems) = refs[-5:-3], refs[-3:]
    cols = outs[0].shape[1]
    waits = load_shards(0, sources, idx_ref, image, got, weights, x_ref, w_ref, sems)
    for k, copies in enumerate(waits):
        for c in copies:
            c.wait()
        for p in range(2):
            part = dot(x_ref[k], w_ref[k, :, p * cols : (p + 1) * cols])
            if k == 0:
                outs[p][...] = part
            else:
                outs[p][...] += part


def finish_kernel(first, source, extra, idx_ref, slots, acc, image, *refs):
    got, weights = refs[:6], refs[6:-7]
    (keep, to_y, to_x, to_both), (x_ref, w_ref, sems) = refs[-7:-3], refs[-3:]
    y = idx_ref[2]
    rows = image.shape[0]
    cols = keep.shape[1]
    kind = to_y.dtype
    waits = load_shards(first, (source,), idx_ref, image, got, weights, x_ref, w_ref, sems)
    for c in waits[0]:
        c.wait()
    total = acc[...] + dot(x_ref[0], w_ref[0])
    low = y == 0
    mine = jnp.where(low, total[:, :cols], total[:, cols:])
    other = jnp.where(low, total[:, cols:], total[:, :cols]).astype(kind)
    keep[...] = mine[: 2 * rows]
    to_y[:rows, :] = other[rows : 2 * rows]
    to_y[rows : 2 * rows, :] = other[:rows]
    to_x[...] = mine[2 * rows :].astype(kind)
    to_both[:rows, :] = other[3 * rows :]
    to_both[rows:, :] = other[2 * rows : 3 * rows]
    if extra:
        n = slots.shape[0]
        to_y[2 * rows : 2 * rows + n, :HD] = slots[...]
        to_y[2 * rows + n :, :] = jnp.zeros((extra - n, cols), kind)
        if cols > HD:
            to_y[2 * rows : 2 * rows + n, HD:] = jnp.zeros((n, cols - HD), kind)


def key_kernel(keep, got_y, got_x, got_both, gain, slots, out):
    rows = keep.shape[0]
    n = slots.shape[0]
    raw = (keep[...] + got_y[:rows, :]) + (got_x[...] + got_both[...])
    for c in range(0, raw.shape[1], HD):
        part = raw[:, c : c + HD]
        scale = lax.rsqrt(jnp.mean(part * part, axis=-1, keepdims=True) + 1e-05)
        out[:rows, c : c + HD] = (part * scale * gain[...]).astype(BF16)
    pad = jnp.zeros((out.shape[0] - rows - 2 * n, HD), F32)
    out[rows:, :HD] = jnp.concatenate([slots[...], got_y[rows : rows + n, :HD], pad], 0).astype(BF16)


def score_kernel(n, heads, q_ref, limit_ref, *refs):
    pieces = refs[:n]
    expo_ref, total_ref, s_ref = refs[n:]
    rows = limit_ref.shape[0]
    piece = s_ref.shape[1] // n
    scale = 1.0 / math.sqrt(HD)
    limit = limit_ref[...]
    top = jnp.full((heads * rows, 1), -1e30, F32)
    for i in range(n):
        slots = pieces[i][piece : piece + 16, :].astype(F32)
        seen = []
        for c in range(piece // HD):
            slot = slots[c : c + 1, :]
            seen.append(jnp.where((slot >= 0.0) & (slot <= limit), 1.0, 0.0))
        seen = jnp.concatenate(seen, 1)
        s = dot_nt(q_ref[...], pieces[i][:piece, :]) * scale
        s = jnp.where(seen[None] > 0.5, s.reshape(heads, rows, piece), -1e30).reshape(heads * rows, piece)
        s_ref[:, i * piece : (i + 1) * piece] = s
        top = jnp.maximum(top, jnp.max(s, axis=1, keepdims=True))
    total = jnp.zeros((heads * rows, 1), F32)
    for i in range(n):
        s = s_ref[:, i * piece : (i + 1) * piece]
        e = jnp.where(s > -1e29, jnp.exp(s - top), 0.0)
        total = total + jnp.sum(e, axis=1, keepdims=True)
        expo_ref[:, i * piece : (i + 1) * piece] = e.astype(BF16)
    total_ref[...] = total


def value_kernel(n, heads, expo_ref, total_ref, *refs):
    values, out_ref = refs[:n], refs[n]
    rows = out_ref.shape[0]
    piece = values[0].shape[0]
    acc = jnp.zeros((heads * rows, HD), F32)
    for i in range(n):
        acc = acc + dot(expo_ref[:, i * piece : (i + 1) * piece], values[i][...])
    attn = (acc / total_ref[...]).astype(BF16)
    for j in range(heads):
        out_ref[:, j * HD : (j + 1) * HD] = attn[j * rows : (j + 1) * rows, :]


def proj_kernel(n, idx_ref, *refs):
    pieces = refs[:n]
    w_ref, keep_ref, send_ref, a_ref, p_ref = refs[n:]
    rows, width = pieces[0].shape
    depth = w_ref.shape[0]
    step = pl.program_id(0)

    @pl.when(step == 0)
    def _():
        for k in range(n):
            at_row = pl.multiple_of(idx_ref[1 + 2 * k] * rows, rows)
            at_col = pl.multiple_of(idx_ref[2 + 2 * k] * width, width)
            a_ref[pl.ds(at_row, rows), pl.ds(at_col, width)] = pieces[k][...]

    part = dot(a_ref[:, pl.ds(pl.multiple_of(step * depth, depth), depth)], w_ref[...])

    @pl.when(step == 0)
    def _():
        p_ref[...] = part

    @pl.when(step > 0)
    def _():
        p_ref[...] += part

    @pl.when(step == pl.num_programs(0) - 1)
    def _():
        size = keep_ref.shape[0]
        core = idx_ref[0]
        keep_ref[...] = p_ref[pl.ds(pl.multiple_of(core * size, size), size), :]
        send_ref[...] = p_ref[pl.ds(pl.multiple_of((1 - core) * size, size), size), :].astype(BF16)


def body(
    image_feats,
    slot_image,
    key_weight,
    value_weight,
    key_gain,
    queries,
    text_image,
    text_hidden,
    out_weight,
    attn_gate,
):
    groups, nblk, cores = (lax.axis_size(a) for a in ("groups", "blk", "heads"))
    lines = nblk // 2
    tok = image_feats.shape[0]
    depth = key_weight.shape[0]
    kv_cols = key_weight.shape[1]
    mine_cols = kv_cols // 2
    text_rows = queries.shape[0]
    q_half = queries.shape[1] // 2
    per_kv = q_half // mine_cols
    grp, blk, core = (lax.axis_index(a) for a in ("groups", "blk", "heads"))
    par = grp % 2
    y = blk % 2
    line = blk // 2

    swap_y = [(b, b ^ 1) for b in range(nblk)]
    swap_core = [(c, c ^ 1) for c in range(cores)]
    half = depth // 2
    fast = lines == 4 and cores == 2 and kv_cols == 2 * HD

    def along(name, array, d, ok=lambda l: True):
        with jax.named_scope(f"{name}_z{d}"):
            return lax.ppermute(array, "blk", [(b, b ^ (2 * d)) for b in range(nblk) if ok(b // 2)])

    def over_y(name, array):
        with jax.named_scope(name + "_y"):
            return lax.ppermute(array, "blk", swap_y)

    def over_core(name, array):
        with jax.named_scope(name + "_core"):
            return lax.ppermute(array, "heads", swap_core)

    def over_x(name, array):
        with jax.named_scope(name + "_x"):
            return lax.ppermute(array, "groups", [(g, g ^ 1) for g in range(groups)])

    def over_both(name, array):
        pairs = [(g * nblk + b, (g ^ 1) * nblk + (b ^ 1)) for g in range(groups) for b in range(nblk)]
        with jax.named_scope(name + "_xy"):
            return lax.ppermute(array, ("groups", "blk"), pairs)

    def hold(*arrays):
        return lax.optimization_barrier(arrays)

    def take_y(array, size, which):
        return lax.dynamic_slice_in_dim(array, which * size, size, 1)

    def middle(l):
        return l in (1, 2)

    half_lines = lines // 2

    def share(to_x, to_y):
        return jnp.concatenate(
            [
                lax.dynamic_slice_in_dim(
                    image_feats, ((2 * (core * half_lines + l) + to_y) * 2 + to_x) * half, half, 1
                )
                for l in range(half_lines)
            ],
            1,
        )

    half_lines = lines // 2
    scalars = pl.BlockSpec(memory_space=pltpu.SMEM)
    share = jax.ShapeDtypeStruct((tok, half_lines * half), BF16)

    def shares(flips, *weights):
        out_shape = [share] * len(flips)
        if weights:
            out_shape.append(jax.ShapeDtypeStruct((2 * half, kv_cols), BF16))
        return pl.pallas_call(
            functools.partial(share_kernel, flips, half_lines),
            out_shape=tuple(out_shape),
            in_specs=[scalars, FREE] + [FREE] * len(weights),
            out_specs=(WHOLE,) * len(out_shape),
            scratch_shapes=[pltpu.SemaphoreType.DMA((2 + len(flips) * half_lines,))],
            compiler_params=pltpu.CompilerParams(vmem_limit_bytes=56 * 1024 * 1024),
        )(jnp.stack([par, core, y]), image_feats, *weights)

    share_x, share_y, own = shares(((1, 0), (0, 1)), key_weight, value_weight)
    (share_both,) = shares(((1, 1),))
    if fast:
        def devices(route):
            pairs = []
            for l in range(lines):
                for yy in range(2):
                    for c in range(cores):
                        to_l, to_y, to_c = route(l, yy, c)
                        pairs.append(((2 * l + yy) * cores + c, (2 * to_l + to_y) * cores + to_c))
            return pairs

        def to_head(name, tile):
            tiles = []
            for r in range(2):
                with jax.named_scope(name + "_head"):
                    tiles.append(
                        lax.ppermute(
                            tile, ("blk", "heads"), devices(lambda l, yy, c: (2 * c + yy, (l % 2) ^ r, l // 2))
                        )
                    )
            return tiles + [over_core(name + "_tile", t) for t in tiles]

        def query_round(queries, r):
            with jax.named_scope("q_head"):
                return lax.ppermute(
                    take_y(queries, q_half, y ^ r),
                    ("blk", "heads"),
                    devices(lambda l, yy, c: (2 * c + (r ^ yy), l % 2, l // 2)),
                )

        z1, zm = along("w", own, 1), along("w", own, 3, middle)
        img_y, img_x = over_y("image", share_y), over_x("image", share_x)
        z1, zm, img_y, img_x, share_both = hold(z1, zm, img_y, img_x, share_both)
        fb, fa = along("w_across", z1, 3, middle), along("w_out", zm, 1, middle)
        img_both = over_both("image", share_both)
        core_y, core_x = over_core("image", img_y), over_core("image", img_x)
        fb, fa, img_both, core_y, core_x = hold(fb, fa, img_both, core_y, core_x)
        core_both = over_core("image", img_both)
        last_k, last_v = along("wk_end", fb[:half], 1, middle), fb[half:]
        refs = [own, z1, fb, fa]
        both = lambda i, o: tuple(((i, at), (o, at)) for at in (0, half))
        sources = (both(0, 0), both(1, 1), both(2, 3))
    else:
        img_y, img_x, img_both = over_y("image", share_y), over_x("image", share_x), over_both("image", share_both)
        core_y, core_x, core_both = (over_core("image", i) for i in (img_y, img_x, img_both))
        refs = [own] + [along("w", own, d) for d in range(1, lines)]
        sources = tuple(tuple(((d, at), (d, at)) for at in (0, half)) for d in range(lines - 1))
    pieces = [img_y, core_y, img_x, core_x, img_both, core_both]
    slots = slot_image.astype(F32).reshape(tok // HD, HD)
    extra = 8 * (-(-(tok // HD) // 8))

    idx = jnp.stack([par, core, y, ((line == 1) | (line == 2)).astype(jnp.int32)] + [line ^ d for d in range(lines)])
    macs = 4 * tok * half * kv_cols
    acc = jax.ShapeDtypeStruct((4 * tok, kv_cols), F32)
    key_acc, value_acc = pl.pallas_call(
        functools.partial(partial_kernel, sources),
        out_shape=(acc, acc),
        in_specs=[scalars] + [FREE] * (7 + len(refs)),
        out_specs=(WHOLE, WHOLE),
        scratch_shapes=[
            pltpu.VMEM((lines - 1, 4 * tok, half), BF16),
            pltpu.VMEM((lines - 1, half, 2 * kv_cols), BF16),
            pltpu.SemaphoreType.DMA((lines - 1, 6)),
        ],
        compiler_params=BIG,
        cost_estimate=pl.CostEstimate(
            flops=4 * macs * (lines - 1), bytes_accessed=macs // 16, transcendentals=0
        ),
    )(idx, image_feats, *pieces, *refs)

    def finish(acc, weights, source, extra, kind):
        out = lambda rows, dtype: jax.ShapeDtypeStruct((rows, mine_cols), dtype)
        return pl.pallas_call(
            functools.partial(finish_kernel, lines - 1, (source,), extra),
            out_shape=(out(2 * tok, F32), out(2 * tok + extra, kind), out(2 * tok, kind), out(2 * tok, kind)),
            in_specs=[scalars, WHOLE, WHOLE] + [FREE] * (7 + len(weights)),
            out_specs=(WHOLE,) * 4,
            scratch_shapes=[
                pltpu.VMEM((1, 4 * tok, half), BF16),
                pltpu.VMEM((1, half, kv_cols), BF16),
                pltpu.SemaphoreType.DMA((1, 5)),
            ],
            compiler_params=BIG,
            cost_estimate=pl.CostEstimate(flops=2 * macs, bytes_accessed=macs // 32, transcendentals=0),
        )(idx, slots, acc, image_feats, *pieces, *weights)

    if fast:
        key_last, value_last = [zm, last_k], None
        key_src, value_src = ((0, 0), (1, 0)), ((0, half), (1, 0))
    else:
        key_last = value_last = refs[-1:]
        key_src, value_src = ((0, 0), (0, 0)), ((0, half), (0, half))
    if fast:
        key_acc, last_k, last_v = hold(key_acc, last_k, last_v)
        key_last = [zm, last_k]
        value_last = [zm, along("wv_end", last_v, 1, middle)]
    keep, to_y, to_x, to_both = finish(key_acc, key_last, key_src, extra, F32)
    if fast:
        to_y, to_x, to_both, queries = hold(to_y, to_x, to_both, queries)
    key_parts = [over_y("key", to_y), over_x("key", to_x), over_both("key", to_both)]
    if fast:
        q_0, q_1 = query_round(queries, 0), query_round(queries, 1)
        *key_parts, q_0, q_1 = hold(*key_parts, q_0, q_1)
    slot_rows = 2 * tok // HD
    packed = pl.pallas_call(
        key_kernel,
        out_shape=jax.ShapeDtypeStruct((2 * tok + slot_rows + (-slot_rows % 16), mine_cols), BF16),
        in_specs=[WHOLE] * 6,
        out_specs=WHOLE,
        compiler_params=PARAMS,
    )(keep, *key_parts, key_gain.reshape(1, HD), slots)

    rows = 2 * text_rows
    if fast:
        is_low = line % 2 == 0
        row_at = 2 * core + y
    else:

        def to_head(name, tile):
            return [tile if d == 0 else along(name, tile, d) for d in range(lines)]

        q_0, q_1 = take_y(queries, q_half, y), over_y("q", take_y(queries, q_half, 1 - y))
        is_low = y == 0
        row_at = line
    q_rows = jnp.concatenate([jnp.where(is_low, q_0, q_1), jnp.where(is_low, q_1, q_0)], 0)
    q_all = q_rows.reshape(rows, per_kv, HD).transpose(1, 0, 2).reshape(per_kv * rows, HD)
    limit = lax.dynamic_slice_in_dim(text_image, row_at * rows, rows, 0).astype(F32).reshape(rows, 1)

    key_pieces = to_head("key", packed)

    tokens = 2 * tok * lines
    expo, total = pl.pallas_call(
        functools.partial(score_kernel, lines, per_kv),
        out_shape=(
            jax.ShapeDtypeStruct((per_kv * rows, tokens), BF16),
            jax.ShapeDtypeStruct((per_kv * rows, 1), F32),
        ),
        in_specs=[WHOLE] * (2 + lines),
        out_specs=(WHOLE, WHOLE),
        scratch_shapes=[pltpu.VMEM((per_kv * rows, tokens), F32)],
        compiler_params=PARAMS,
    )(q_all, limit, *key_pieces)

    keep, to_y, to_x, to_both = finish(value_acc, value_last, value_src, 0, BF16)
    value_parts = [over_y("value", to_y), over_x("value", to_x), over_both("value", to_both)]
    value_y, value_x, value_both = (part.astype(F32) for part in value_parts)
    values = ((keep + value_y) + (value_x + value_both)).astype(BF16)
    value_pieces = to_head("value", values)

    attn = pl.pallas_call(
        functools.partial(value_kernel, lines, per_kv),
        out_shape=jax.ShapeDtypeStruct((rows, q_half), BF16),
        in_specs=[WHOLE] * (2 + lines),
        out_specs=WHOLE,
        compiler_params=PARAMS,
    )(expo, total, *value_pieces)

    where = []
    if fast:
        mine = []
        for k in range(lines):
            pairs = devices(lambda l, yy, c: ((2 * (l % 2) + c) ^ k, yy, l // 2))
            with jax.named_scope(f"attn_out{k}"):
                mine.append(lax.ppermute(attn, ("blk", "heads"), pairs))
            where.append((2 * ((line ^ k) % 2), (line ^ k) // 2))
        where = [(at + y, col) for at, col in where] + [(at + 1 - y, col) for at, col in where]
    else:
        mine = [attn if d == 0 else along("attn", attn, d) for d in range(lines)]
        where = [(line ^ d, y) for d in range(lines)] + [(line ^ d, 1 - y) for d in range(lines)]
    other = [over_y(f"attn{d}", m) for d, m in enumerate(mine)]

    out_rows = lines * rows
    out_cols = out_weight.shape[1]
    steps = 4
    out_spec = pl.BlockSpec((out_rows // 2, out_cols), lambda i, s: (0, 0))
    keep, send = pl.pallas_call(
        functools.partial(proj_kernel, 2 * lines),
        out_shape=(
            jax.ShapeDtypeStruct((out_rows // 2, out_cols), F32),
            jax.ShapeDtypeStruct((out_rows // 2, out_cols), BF16),
        ),
        grid_spec=pltpu.PrefetchScalarGridSpec(
            num_scalar_prefetch=1,
            grid=(steps,),
            in_specs=[pl.BlockSpec((rows, q_half), lambda i, s: (0, 0))] * (2 * lines)
            + [pl.BlockSpec((2 * q_half // steps, out_cols), lambda i, s: (i, 0))],
            out_specs=(out_spec, out_spec),
            scratch_shapes=[pltpu.VMEM((out_rows, 2 * q_half), BF16), pltpu.VMEM((out_rows, out_cols), F32)],
        ),
        compiler_params=BIG,
    )(jnp.stack([core] + [i for pair in where for i in pair]), *mine, *other, out_weight)
    head_total = keep + over_core("proj", send).astype(F32)
    return (text_hidden.astype(F32) + jnp.tanh(attn_gate[0]) * head_total).astype(BF16)


def solution(mesh):
    placed = (
        P(("groups", "blk"), None),
        P(("groups", "blk")),
        P("blk", "heads"),
        P("blk", "heads"),
        P(),
        P(("groups", "blk"), "heads"),
        P("groups"),
        P(("groups", "heads"), "blk"),
        P("heads", "blk"),
        P(),
    )
    return jax.shard_map(
        body, mesh=mesh, in_specs=placed, out_specs=P(("groups", "heads"), "blk"), check_vma=False
    )
```

```python
import functools
import math

import jax
import jax.numpy as jnp
from jax import lax
from jax.experimental import pallas as pl
from jax.experimental.pallas import tpu as pltpu
from jax.sharding import PartitionSpec as P

HD = 128
F32 = jnp.float32
BF16 = jnp.bfloat16
VMEM_BYTES = 20 * 1024 * 1024
PARAMS = pltpu.CompilerParams(vmem_limit_bytes=VMEM_BYTES)
BIG = pltpu.CompilerParams(vmem_limit_bytes=52 * 1024 * 1024)
WHOLE = pl.BlockSpec(memory_space=pltpu.VMEM)
FREE = pl.BlockSpec(memory_space=pltpu.HBM)


def dot(a, b):
    return jnp.dot(a, b, preferred_element_type=F32)


def dot_nt(a, b):
    return lax.dot_general(a, b, (((1,), (1,)), ((), ())), preferred_element_type=F32)


def share_kernel(flips, half_lines, image, *refs):
    par, core, y = lax.axis_index("groups") % 2, lax.axis_index("heads"), lax.axis_index("blk") % 2
    n = len(flips)
    n_weights = (len(refs) - n - 1) // 2
    weights, outs, sems = refs[:n_weights], refs[n_weights:-1], refs[-1]
    copies = []
    for weight, own in zip(weights, outs[n:]):
        half = own.shape[0]
        copies.append((weight.at[pl.ds(pl.multiple_of(par * half, half), half), :], own))
    for (flip_x, flip_y), out in zip(flips, outs):
        half = out.shape[1] // half_lines
        to_par = 1 - par if flip_x else par
        to_y = 1 - y if flip_y else y
        for l in range(half_lines):
            at = pl.multiple_of(((2 * (core * half_lines + l) + to_y) * 2 + to_par) * half, half)
            copies.append((image.at[:, pl.ds(at, half)], out.at[:, pl.ds(l * half, half)]))
    copies = [pltpu.make_async_copy(src, dst, sems.at[i]) for i, (src, dst) in enumerate(copies)]
    for c in copies:
        c.start()
    for c in copies:
        c.wait()


def load_shards(first, sources, idx_ref, image, got, weights, x_ref, w_ref, sems):
    par, core, y, inner = idx_ref[0], idx_ref[1], idx_ref[2], idx_ref[3]
    rows = image.shape[0]
    half = x_ref.shape[2]
    half_lines = got[0].shape[1] // half
    cols = weights[0].shape[1]

    def copy(src, dst, k, i):
        return pltpu.make_async_copy(src, dst, sems.at[k, i])

    waits = []
    for k, projections in enumerate(sources):
        line = idx_ref[4 + first + k]
        own_at = pl.multiple_of(((2 * line + y) * 2 + par) * half, half)
        here = line // half_lines == core
        got_at = pl.multiple_of(lax.rem(line, half_lines) * half, half)
        own = copy(image.at[:, pl.ds(own_at, half)], x_ref.at[k, pl.ds(0, rows), :], k, 0)
        own.start()

        def from_core(which, k=k, got_at=got_at):
            return [
                copy(
                    got[2 * i + which].at[:, pl.ds(got_at, half)],
                    x_ref.at[k, pl.ds((i + 1) * rows, rows), :],
                    k,
                    1 + i,
                )
                for i in range(3)
            ]

        mine = from_core(0)

        @pl.when(here)
        def _(mine=mine):
            for c in mine:
                c.start()

        @pl.when(jnp.logical_not(here))
        def _(from_core=from_core):
            for c in from_core(1):
                c.start()

        waits.append([own] + mine)
        for p, (in_src, out_src) in enumerate(projections):

            def from_weight(src, k=k, p=p):
                return copy(
                    weights[src[0]].at[pl.ds(src[1], half), :], w_ref.at[k, :, pl.ds(p * cols, cols)], k, 4 + p
                )

            weight = from_weight(in_src)
            if in_src == out_src:
                weight.start()
            else:

                @pl.when(inner > 0)
                def _(weight=weight):
                    weight.start()

                @pl.when(inner <= 0)
                def _(from_weight=from_weight, out_src=out_src):
                    from_weight(out_src).start()

            waits[-1].append(weight)
    return waits


def project_kernel(sources, extra, idx_ref, slots, image, *refs):
    got, weights = refs[:6], refs[6:-8]
    (keep, to_y, to_x, to_both), (x_ref, w_ref, acc_ref, sems) = refs[-8:-4], refs[-4:]
    y = idx_ref[2]
    rows = image.shape[0]
    cols = keep.shape[1]
    kind = to_y.dtype
    waits = load_shards(0, tuple((s,) for s in sources), idx_ref, image, got, weights, x_ref, w_ref, sems)
    for k, copies in enumerate(waits):
        for c in copies:
            c.wait()
        part = dot(x_ref[k], w_ref[k])
        if k == 0:
            acc_ref[...] = part
        elif k < len(waits) - 1:
            acc_ref[...] += part
    total = acc_ref[...] + part
    low = y == 0
    mine = jnp.where(low, total[:, :cols], total[:, cols:])
    other = jnp.where(low, total[:, cols:], total[:, :cols]).astype(kind)
    keep[...] = mine[: 2 * rows]
    to_y[:rows, :] = other[rows : 2 * rows]
    to_y[rows : 2 * rows, :] = other[:rows]
    to_x[...] = mine[2 * rows :].astype(kind)
    to_both[:rows, :] = other[3 * rows :]
    to_both[rows:, :] = other[2 * rows : 3 * rows]
    if extra:
        n = slots.shape[0]
        to_y[2 * rows : 2 * rows + n, :HD] = slots[...]
        to_y[2 * rows + n :, :] = jnp.zeros((extra - n, cols), kind)
        if cols > HD:
            to_y[2 * rows : 2 * rows + n, HD:] = jnp.zeros((n, cols - HD), kind)


def key_kernel(keep, got_y, got_x, got_both, gain, slots, out):
    rows = keep.shape[0]
    n = slots.shape[0]
    raw = (keep[...] + got_y[:rows, :]) + (got_x[...] + got_both[...])
    for c in range(0, raw.shape[1], HD):
        part = raw[:, c : c + HD]
        scale = lax.rsqrt(jnp.mean(part * part, axis=-1, keepdims=True) + 1e-05)
        out[:rows, c : c + HD] = (part * scale * gain[...]).astype(BF16)
    pad = jnp.zeros((out.shape[0] - rows - 2 * n, HD), F32)
    out[rows:, :HD] = jnp.concatenate([slots[...], got_y[rows : rows + n, :HD], pad], 0).astype(BF16)


def score_kernel(n, heads, limit_ref, keys_ref, *refs):
    queries = refs[:n]
    expo_ref, figures_ref, q_ref = refs[n:]
    rows = queries[0].shape[0]
    tokens = expo_ref.shape[1]
    scale = 1.0 / math.sqrt(HD)
    slots = keys_ref[tokens : tokens + 16 * (-(-tokens // HD) // 16 + (-(-tokens // HD) % 16 > 0)), :].astype(F32)
    lane = lax.broadcasted_iota(jnp.int32, (rows, HD), 1)
    for i in range(n):
        limit = limit_ref[i * rows : (i + 1) * rows, :]
        seen = []
        for c in range(tokens // HD):
            slot = slots[c : c + 1, :]
            seen.append(jnp.where((slot >= 0.0) & (slot <= limit), 1.0, 0.0))
        seen = jnp.concatenate(seen, 1)
        for j in range(heads):
            q_ref[j * rows : (j + 1) * rows, :] = queries[i][:, j * HD : (j + 1) * HD]
        s = dot_nt(q_ref[...], keys_ref[:tokens, :]) * scale
        s = jnp.where(seen[None] > 0.5, s.reshape(heads, rows, tokens), -1e30).reshape(heads * rows, tokens)
        top = jnp.max(s, axis=1, keepdims=True).astype(BF16).astype(F32)
        e = jnp.where(s > -1e29, jnp.exp(s - top), 0.0)
        total = jnp.sum(e, axis=1, keepdims=True)
        expo_ref[i * heads * rows : (i + 1) * heads * rows, :] = e.astype(BF16)
        high = total.astype(BF16).astype(F32)
        figures = jnp.zeros((rows, HD), F32)
        for j in range(heads):
            part = slice(j * rows, (j + 1) * rows)
            figures = jnp.where(lane == j, top[part], figures)
            figures = jnp.where(lane == heads + j, high[part], figures)
            figures = jnp.where(lane == 2 * heads + j, total[part] - high[part], figures)
        figures_ref[i * rows : (i + 1) * rows, :] = figures.astype(BF16)


def value_kernel(n, heads, expo_ref, figures_ref, values_ref, *outs):
    rows = figures_ref.shape[0] // n
    for i in range(n):
        acc = dot(expo_ref[i * heads * rows : (i + 1) * heads * rows, :], values_ref[...]).astype(BF16)
        for j in range(heads):
            outs[i][:, j * HD : (j + 1) * HD] = acc[j * rows : (j + 1) * rows, :]
        outs[i][:, heads * HD :] = figures_ref[i * rows : (i + 1) * rows, :]


def combine_kernel(n, heads, *refs):
    parts, out_ref = refs[:n], refs[n]
    rows = out_ref.shape[0]
    lane = lax.broadcasted_iota(jnp.int32, (rows, HD), 1)
    figures = [part[:, heads * HD :].astype(F32) for part in parts]

    def column(figure, at):
        return jnp.sum(jnp.where(lane == at, figure, 0.0), axis=1, keepdims=True)

    for j in range(heads):
        tops = [column(f, j) for f in figures]
        top = functools.reduce(jnp.maximum, tops)
        total = jnp.zeros((rows, 1), F32)
        acc = jnp.zeros((rows, HD), F32)
        for part, figure, own_top in zip(parts, figures, tops):
            weight = jnp.exp(own_top - top)
            total = total + weight * (column(figure, heads + j) + column(figure, 2 * heads + j))
            acc = acc + weight * part[:, j * HD : (j + 1) * HD].astype(F32)
        out_ref[:, j * HD : (j + 1) * HD] = (acc / total).astype(BF16)


def proj_kernel(n, idx_ref, *refs):
    pieces = refs[:n]
    w_ref, keep_ref, send_ref, a_ref, p_ref = refs[n:]
    rows, width = pieces[0].shape
    for k in range(n):
        at_row = pl.multiple_of(idx_ref[1 + 2 * k] * rows, rows)
        at_col = pl.multiple_of(idx_ref[2 + 2 * k] * width, width)
        a_ref[pl.ds(at_row, rows), pl.ds(at_col, width)] = pieces[k][...]
    p_ref[...] = dot(a_ref[...], w_ref[...])
    size = keep_ref.shape[0]
    core = idx_ref[0]
    keep_ref[...] = p_ref[pl.ds(pl.multiple_of(core * size, size), size), :]
    send_ref[...] = p_ref[pl.ds(pl.multiple_of((1 - core) * size, size), size), :].astype(BF16)


def body(
    image_feats,
    slot_image,
    key_weight,
    value_weight,
    key_gain,
    queries,
    text_image,
    text_hidden,
    out_weight,
    attn_gate,
):
    groups, nblk, cores = (lax.axis_size(a) for a in ("groups", "blk", "heads"))
    lines = nblk // 2
    tok = image_feats.shape[0]
    depth = key_weight.shape[0]
    kv_cols = key_weight.shape[1]
    mine_cols = kv_cols // 2
    text_rows = queries.shape[0]
    q_half = queries.shape[1] // 2
    per_kv = q_half // mine_cols
    grp, blk, core = (lax.axis_index(a) for a in ("groups", "blk", "heads"))
    par = grp % 2
    y = blk % 2
    line = blk // 2

    swap_y = [(b, b ^ 1) for b in range(nblk)]
    swap_core = [(c, c ^ 1) for c in range(cores)]
    half = depth // 2
    fast = lines == 4 and cores == 2 and kv_cols == 2 * HD

    def along(name, array, d, ok=lambda l: True):
        with jax.named_scope(f"{name}_z{d}"):
            return lax.ppermute(array, "blk", [(b, b ^ (2 * d)) for b in range(nblk) if ok(b // 2)])

    def over_y(name, array):
        with jax.named_scope(name + "_y"):
            return lax.ppermute(array, "blk", swap_y)

    def over_core(name, array):
        with jax.named_scope(name + "_core"):
            return lax.ppermute(array, "heads", swap_core)

    def over_x(name, array):
        with jax.named_scope(name + "_x"):
            return lax.ppermute(array, "groups", [(g, g ^ 1) for g in range(groups)])

    def over_both(name, array):
        pairs = [(g * nblk + b, (g ^ 1) * nblk + (b ^ 1)) for g in range(groups) for b in range(nblk)]
        with jax.named_scope(name + "_xy"):
            return lax.ppermute(array, ("groups", "blk"), pairs)

    def hold(*arrays):
        return lax.optimization_barrier(arrays)

    def take_y(array, size, which):
        return lax.dynamic_slice_in_dim(array, which * size, size, 1)

    def middle(l):
        return l in (1, 2)

    half_lines = lines // 2

    def share(to_x, to_y):
        return jnp.concatenate(
            [
                lax.dynamic_slice_in_dim(
                    image_feats, ((2 * (core * half_lines + l) + to_y) * 2 + to_x) * half, half, 1
                )
                for l in range(half_lines)
            ],
            1,
        )

    half_lines = lines // 2
    scalars = pl.BlockSpec(memory_space=pltpu.SMEM)
    share = jax.ShapeDtypeStruct((tok, half_lines * half), BF16)

    def shares(flips, *weights):
        out_shape = [share] * len(flips) + [jax.ShapeDtypeStruct((half, kv_cols), BF16)] * len(weights)
        return pl.pallas_call(
            functools.partial(share_kernel, flips, half_lines),
            out_shape=tuple(out_shape),
            in_specs=[FREE] + [FREE] * len(weights),
            out_specs=(WHOLE,) * len(out_shape),
            scratch_shapes=[pltpu.SemaphoreType.DMA((2 + len(flips) * half_lines,))],
            compiler_params=pltpu.CompilerParams(vmem_limit_bytes=56 * 1024 * 1024),
        )(image_feats, *weights)

    share_x, share_y, key_own = shares(((1, 0), (0, 1)), key_weight)
    share_both, value_own = shares(((1, 1),), value_weight)
    if fast:
        def devices(route):
            pairs = []
            for l in range(lines):
                for yy in range(2):
                    for c in range(cores):
                        to_l, to_y, to_c = route(l, yy, c)
                        pairs.append(((2 * l + yy) * cores + c, (2 * to_l + to_y) * cores + to_c))
            return pairs

        def to_head(name, tile):
            tiles = []
            for r in range(2):
                with jax.named_scope(name + "_head"):
                    tiles.append(
                        lax.ppermute(
                            tile, ("blk", "heads"), devices(lambda l, yy, c: (2 * c + yy, (l % 2) ^ r, l // 2))
                        )
                    )
            return tiles + [over_core(name + "_tile", t) for t in tiles]

        k1, km = along("wk", key_own, 1), along("wk", key_own, 3, middle)
        img_y, img_x = over_y("image", share_y), over_x("image", share_x)
        kb, ka = along("wk_across", k1, 3, middle), along("wk_out", km, 1, middle)
        kb, ka, img_y, img_x, share_both, value_own = hold(kb, ka, img_y, img_x, share_both, value_own)
        img_both = over_both("image", share_both)
        ke = along("wk_end", kb, 1, middle)
        v1, vm = along("wv", value_own, 1), along("wv", value_own, 3, middle)
        core_y, core_x = over_core("image", img_y), over_core("image", img_x)
        v1, vm, ke, img_both, core_y, core_x = hold(v1, vm, ke, img_both, core_y, core_x)
        core_both = over_core("image", img_both)
        vb, va = along("wv_across", v1, 3, middle), along("wv_out", vm, 1, middle)
        pass
        key_refs, value_refs = [key_own, k1, kb, ka, km, ke], [value_own, v1, vb, va, vm]
        pair = lambda i, o: ((i, 0), (o, 0))
        sources = (pair(0, 0), pair(1, 1), pair(2, 3), pair(4, 5))
    else:
        img_y, img_x, img_both = over_y("image", share_y), over_x("image", share_x), over_both("image", share_both)
        core_y, core_x, core_both = (over_core("image", i) for i in (img_y, img_x, img_both))
        key_refs = [key_own] + [along("wk", key_own, d) for d in range(1, lines)]
        value_refs = [value_own] + [along("wv", value_own, d) for d in range(1, lines)]
        sources = tuple(((d, 0), (d, 0)) for d in range(lines))
    pieces = [img_y, core_y, img_x, core_x, img_both, core_both]
    slots = slot_image.astype(F32).reshape(tok // HD, HD)
    extra = 8 * (-(-(tok // HD) // 8))

    idx = jnp.stack([par, core, y, ((line == 1) | (line == 2)).astype(jnp.int32)] + [line ^ d for d in range(lines)])
    macs = 4 * tok * half * kv_cols

    def project(weights, extra, kind):
        out = lambda rows, dtype: jax.ShapeDtypeStruct((rows, mine_cols), dtype)
        return pl.pallas_call(
            functools.partial(project_kernel, sources, extra),
            out_shape=(out(2 * tok, F32), out(2 * tok + extra, kind), out(2 * tok, kind), out(2 * tok, kind)),
            in_specs=[scalars, WHOLE] + [FREE] * (7 + len(weights)),
            out_specs=(WHOLE,) * 4,
            scratch_shapes=[
                pltpu.VMEM((lines, 4 * tok, half), BF16),
                pltpu.VMEM((lines, half, kv_cols), BF16),
                pltpu.VMEM((4 * tok, kv_cols), F32),
                pltpu.SemaphoreType.DMA((lines, 5)),
            ],
            compiler_params=BIG,
            cost_estimate=pl.CostEstimate(
                flops=2 * macs * lines, bytes_accessed=macs * lines // 32, transcendentals=0
            ),
        )(idx, slots, image_feats, *pieces, *weights)

    rows = 2 * text_rows
    q_mine, q_got = take_y(queries, q_half, y), over_y("q", take_y(queries, q_half, 1 - y))
    low_y = y == 0
    q_rows = jnp.concatenate([jnp.where(low_y, q_mine, q_got), jnp.where(low_y, q_got, q_mine)], 0)
    keep, to_y, to_x, to_both = project(key_refs, extra, F32)
    if fast:
        vb, to_y, to_x, to_both = hold(vb, to_y, to_x, to_both)
    key_parts = [over_y("key", to_y), over_x("key", to_x), over_both("key", to_both)]
    q_pieces = [q_rows if d == 0 else along("q", q_rows, d) for d in range(lines)]
    if fast:
        value_refs.append(along("wv_end", vb, 1, middle))
    slot_rows = 2 * tok // HD
    packed = pl.pallas_call(
        key_kernel,
        out_shape=jax.ShapeDtypeStruct((2 * tok + slot_rows + (-slot_rows % 16), mine_cols), BF16),
        in_specs=[WHOLE] * 6,
        out_specs=WHOLE,
        compiler_params=PARAMS,
    )(keep, *key_parts, key_gain.reshape(1, HD), slots)

    keep, to_y, to_x, to_both = project(value_refs, 0, BF16)
    if fast:
        to_y, to_x, to_both, *q_pieces = hold(to_y, to_x, to_both, *q_pieces)
    value_parts = [over_y("value", to_y), over_x("value", to_x), over_both("value", to_both)]
    limits = text_image.astype(F32).reshape(lines, rows)
    limits = jnp.concatenate([lax.dynamic_slice_in_dim(limits, line ^ d, 1, 0) for d in range(lines)], 0)
    limits = limits.reshape(lines * rows, 1)
    all_rows = lines * rows * per_kv
    expo, figures = pl.pallas_call(
        functools.partial(score_kernel, lines, per_kv),
        out_shape=(
            jax.ShapeDtypeStruct((all_rows, 2 * tok), BF16),
            jax.ShapeDtypeStruct((lines * rows, HD), BF16),
        ),
        in_specs=[WHOLE] * (2 + lines),
        out_specs=(WHOLE, WHOLE),
        scratch_shapes=[pltpu.VMEM((per_kv * rows, HD), BF16)],
        compiler_params=PARAMS,
    )(limits, packed, *q_pieces)
    value_y, value_x, value_both = (part.astype(F32) for part in value_parts)
    values = ((keep + value_y) + (value_x + value_both)).astype(BF16)
    sums = pl.pallas_call(
        functools.partial(value_kernel, lines, per_kv),
        out_shape=(jax.ShapeDtypeStruct((rows, q_half + HD), BF16),) * lines,
        in_specs=[WHOLE] * 3,
        out_specs=(WHOLE,) * lines,
        compiler_params=PARAMS,
    )(expo, figures, values)
    sums = [sums[0]] + [along("sums", sums[d], d) for d in range(1, lines)]
    attn = pl.pallas_call(
        functools.partial(combine_kernel, lines, per_kv),
        out_shape=jax.ShapeDtypeStruct((rows, q_half), BF16),
        in_specs=[WHOLE] * lines,
        out_specs=WHOLE,
        compiler_params=PARAMS,
    )(*sums)
    mine = [attn if d == 0 else along("attn", attn, d) for d in range(lines)]
    where = [(line ^ d, y) for d in range(lines)] + [(line ^ d, 1 - y) for d in range(lines)]
    other = [over_y(f"attn{d}", m) for d, m in enumerate(mine)]

    out_rows = lines * rows
    out_cols = out_weight.shape[1]
    keep, send = pl.pallas_call(
        functools.partial(proj_kernel, 2 * lines),
        out_shape=(
            jax.ShapeDtypeStruct((out_rows // 2, out_cols), F32),
            jax.ShapeDtypeStruct((out_rows // 2, out_cols), BF16),
        ),
        in_specs=[scalars] + [WHOLE] * (2 * lines + 1),
        out_specs=(WHOLE, WHOLE),
        scratch_shapes=[pltpu.VMEM((out_rows, 2 * q_half), BF16), pltpu.VMEM((out_rows, out_cols), F32)],
        compiler_params=PARAMS,
    )(jnp.stack([core] + [i for pair in where for i in pair]), *mine, *other, out_weight)
    head_total = keep + over_core("proj", send).astype(F32)
    return (text_hidden.astype(F32) + jnp.tanh(attn_gate[0]) * head_total).astype(BF16)


def solution(mesh):
    placed = (
        P(("groups", "blk"), None),
        P(("groups", "blk")),
        P("blk", "heads"),
        P("blk", "heads"),
        P(),
        P(("groups", "blk"), "heads"),
        P("groups"),
        P(("groups", "heads"), "blk"),
        P("heads", "blk"),
        P(),
    )
    return jax.shard_map(
        body, mesh=mesh, in_specs=placed, out_specs=P(("groups", "heads"), "blk"), check_vma=False
    )
```

```python
import functools
import math

import jax
import jax.numpy as jnp
from jax import lax
from jax.experimental import pallas as pl
from jax.experimental.pallas import tpu as pltpu
from jax.sharding import PartitionSpec as P

HD = 128
F32 = jnp.float32
BF16 = jnp.bfloat16
VMEM_BYTES = 20 * 1024 * 1024
PARAMS = pltpu.CompilerParams(vmem_limit_bytes=VMEM_BYTES)
BIG = pltpu.CompilerParams(vmem_limit_bytes=52 * 1024 * 1024)
WHOLE = pl.BlockSpec(memory_space=pltpu.VMEM)
FREE = pl.BlockSpec(memory_space=pltpu.HBM)


def dot(a, b):
    return jnp.dot(a, b, preferred_element_type=F32)


def dot_nt(a, b):
    return lax.dot_general(a, b, (((1,), (1,)), ((), ())), preferred_element_type=F32)


def share_kernel(flips, half_lines, image, *refs):
    par, core, y = lax.axis_index("groups") % 2, lax.axis_index("heads"), lax.axis_index("blk") % 2
    n = len(flips)
    n_weights = (len(refs) - n - 1) // 2
    weights, outs, sems = refs[:n_weights], refs[n_weights:-1], refs[-1]
    copies = []
    for weight, own in zip(weights, outs[n:]):
        half = own.shape[0]
        copies.append((weight.at[pl.ds(pl.multiple_of(par * half, half), half), :], own))
    for (flip_x, flip_y), out in zip(flips, outs):
        half = out.shape[1] // half_lines
        to_par = 1 - par if flip_x else par
        to_y = 1 - y if flip_y else y
        for l in range(half_lines):
            at = pl.multiple_of(((2 * (core * half_lines + l) + to_y) * 2 + to_par) * half, half)
            copies.append((image.at[:, pl.ds(at, half)], out.at[:, pl.ds(l * half, half)]))
    copies = [pltpu.make_async_copy(src, dst, sems.at[i]) for i, (src, dst) in enumerate(copies)]
    for c in copies:
        c.start()
    for c in copies:
        c.wait()


def load_shards(first, sources, idx_ref, image, got, weights, x_ref, w_ref, sems):
    par, core, y, inner = idx_ref[0], idx_ref[1], idx_ref[2], idx_ref[3]
    rows = image.shape[0]
    half = x_ref.shape[2]
    half_lines = got[0].shape[1] // half
    cols = weights[0].shape[1]

    def copy(src, dst, k, i):
        return pltpu.make_async_copy(src, dst, sems.at[k, i])

    waits = []
    for k, projections in enumerate(sources):
        line = idx_ref[4 + first + k]
        own_at = pl.multiple_of(((2 * line + y) * 2 + par) * half, half)
        here = line // half_lines == core
        got_at = pl.multiple_of(lax.rem(line, half_lines) * half, half)
        own = copy(image.at[:, pl.ds(own_at, half)], x_ref.at[k, pl.ds(0, rows), :], k, 0)
        own.start()

        def from_core(which, k=k, got_at=got_at):
            return [
                copy(
                    got[2 * i + which].at[:, pl.ds(got_at, half)],
                    x_ref.at[k, pl.ds((i + 1) * rows, rows), :],
                    k,
                    1 + i,
                )
                for i in range(3)
            ]

        mine = from_core(0)

        @pl.when(here)
        def _(mine=mine):
            for c in mine:
                c.start()

        @pl.when(jnp.logical_not(here))
        def _(from_core=from_core):
            for c in from_core(1):
                c.start()

        waits.append([own] + mine)
        for p, (in_src, out_src) in enumerate(projections):

            def from_weight(src, k=k, p=p):
                return copy(
                    weights[src[0]].at[pl.ds(src[1], half), :], w_ref.at[k, :, pl.ds(p * cols, cols)], k, 4 + p
                )

            weight = from_weight(in_src)
            if in_src == out_src:
                weight.start()
            else:

                @pl.when(inner > 0)
                def _(weight=weight):
                    weight.start()

                @pl.when(inner <= 0)
                def _(from_weight=from_weight, out_src=out_src):
                    from_weight(out_src).start()

            waits[-1].append(weight)
    return waits


def project_kernel(sources, extra, idx_ref, slots, image, *refs):
    got, weights = refs[:6], refs[6:-8]
    (keep, to_y, to_x, to_both), (x_ref, w_ref, acc_ref, sems) = refs[-8:-4], refs[-4:]
    y = idx_ref[2]
    rows = image.shape[0]
    cols = keep.shape[1]
    kind = to_y.dtype
    waits = load_shards(0, tuple((s,) for s in sources), idx_ref, image, got, weights, x_ref, w_ref, sems)
    for k, copies in enumerate(waits):
        for c in copies:
            c.wait()
        part = dot(x_ref[k], w_ref[k])
        if k == 0:
            acc_ref[...] = part
        elif k < len(waits) - 1:
            acc_ref[...] += part
    total = acc_ref[...] + part
    low = y == 0
    mine = jnp.where(low, total[:, :cols], total[:, cols:])
    other = jnp.where(low, total[:, cols:], total[:, :cols]).astype(kind)
    keep[...] = mine[: 2 * rows]
    to_y[:rows, :] = other[rows : 2 * rows]
    to_y[rows : 2 * rows, :] = other[:rows]
    to_x[...] = mine[2 * rows :].astype(kind)
    to_both[:rows, :] = other[3 * rows :]
    to_both[rows:, :] = other[2 * rows : 3 * rows]
    if extra:
        n = slots.shape[0]
        to_y[2 * rows : 2 * rows + n, :HD] = slots[...]
        to_y[2 * rows + n :, :] = jnp.zeros((extra - n, cols), kind)
        if cols > HD:
            to_y[2 * rows : 2 * rows + n, HD:] = jnp.zeros((n, cols - HD), kind)


def key_kernel(keep, got_y, got_x, got_both, gain, slots, out):
    rows = keep.shape[0]
    n = slots.shape[0]
    raw = (keep[...] + got_y[:rows, :]) + (got_x[...] + got_both[...])
    for c in range(0, raw.shape[1], HD):
        part = raw[:, c : c + HD]
        scale = lax.rsqrt(jnp.mean(part * part, axis=-1, keepdims=True) + 1e-05)
        out[:rows, c : c + HD] = (part * scale * gain[...]).astype(BF16)
    pad = jnp.zeros((out.shape[0] - rows - 2 * n, HD), F32)
    out[rows:, :HD] = jnp.concatenate([slots[...], got_y[rows : rows + n, :HD], pad], 0).astype(BF16)


def score_kernel(n, heads, limit_ref, keys_ref, *refs):
    *queries, expo_ref, figures_ref, q_ref = refs
    rows = limit_ref.shape[0] // n
    each = n // len(queries)
    tokens = expo_ref.shape[1]
    scale = 1.0 / math.sqrt(HD)
    slots = keys_ref[tokens : tokens + 16 * (-(-tokens // HD) // 16 + (-(-tokens // HD) % 16 > 0)), :].astype(F32)
    lane = lax.broadcasted_iota(jnp.int32, (rows, HD), 1)
    for i in range(n):
        limit = limit_ref[i * rows : (i + 1) * rows, :]
        seen = []
        for c in range(tokens // HD):
            slot = slots[c : c + 1, :]
            seen.append(jnp.where((slot >= 0.0) & (slot <= limit), 1.0, 0.0))
        seen = jnp.concatenate(seen, 1)
        for j in range(heads):
            at = i % each * rows
            q_ref[j * rows : (j + 1) * rows, :] = queries[i // each][at : at + rows, j * HD : (j + 1) * HD]
        s = dot_nt(q_ref[...], keys_ref[:tokens, :]) * scale
        s = jnp.where(seen[None] > 0.5, s.reshape(heads, rows, tokens), -1e30).reshape(heads * rows, tokens)
        top = jnp.max(s, axis=1, keepdims=True).astype(BF16).astype(F32)
        e = jnp.where(s > -1e29, jnp.exp(s - top), 0.0)
        total = jnp.sum(e, axis=1, keepdims=True)
        expo_ref[i * heads * rows : (i + 1) * heads * rows, :] = e.astype(BF16)
        high = total.astype(BF16).astype(F32)
        figures = jnp.zeros((rows, HD), F32)
        for j in range(heads):
            part = slice(j * rows, (j + 1) * rows)
            figures = jnp.where(lane == j, top[part], figures)
            figures = jnp.where(lane == heads + j, high[part], figures)
            figures = jnp.where(lane == 2 * heads + j, total[part] - high[part], figures)
        figures_ref[i * rows : (i + 1) * rows, :] = figures.astype(BF16)


def value_kernel(n, heads, expo_ref, figures_ref, values_ref, *outs):
    rows = figures_ref.shape[0] // n
    for i in range(n):
        acc = dot(expo_ref[i * heads * rows : (i + 1) * heads * rows, :], values_ref[...]).astype(BF16)
        for j in range(heads):
            outs[i][:, j * HD : (j + 1) * HD] = acc[j * rows : (j + 1) * rows, :]
        outs[i][:, heads * HD :] = figures_ref[i * rows : (i + 1) * rows, :]


def combine_kernel(n, heads, *refs):
    parts, out_ref = refs[:n], refs[n]
    rows = out_ref.shape[0]
    lane = lax.broadcasted_iota(jnp.int32, (rows, HD), 1)
    figures = [part[:, heads * HD :].astype(F32) for part in parts]

    def column(figure, at):
        return jnp.sum(jnp.where(lane == at, figure, 0.0), axis=1, keepdims=True)

    for j in range(heads):
        tops = [column(f, j) for f in figures]
        top = functools.reduce(jnp.maximum, tops)
        total = jnp.zeros((rows, 1), F32)
        acc = jnp.zeros((rows, HD), F32)
        for part, figure, own_top in zip(parts, figures, tops):
            weight = jnp.exp(own_top - top)
            total = total + weight * (column(figure, heads + j) + column(figure, 2 * heads + j))
            acc = acc + weight * part[:, j * HD : (j + 1) * HD].astype(F32)
        out_ref[:, j * HD : (j + 1) * HD] = (acc / total).astype(BF16)


def proj_kernel(n, idx_ref, *refs):
    pieces = refs[:n]
    w_ref, keep_ref, send_ref, a_ref, p_ref = refs[n:]
    rows, width = pieces[0].shape
    for k in range(n):
        at_row = pl.multiple_of(idx_ref[1 + 2 * k] * rows, rows)
        at_col = pl.multiple_of(idx_ref[2 + 2 * k] * width, width)
        a_ref[pl.ds(at_row, rows), pl.ds(at_col, width)] = pieces[k][...]
    p_ref[...] = dot(a_ref[...], w_ref[...])
    size = keep_ref.shape[0]
    core = idx_ref[0]
    keep_ref[...] = p_ref[pl.ds(pl.multiple_of(core * size, size), size), :]
    send_ref[...] = p_ref[pl.ds(pl.multiple_of((1 - core) * size, size), size), :].astype(BF16)


def body(
    image_feats,
    slot_image,
    key_weight,
    value_weight,
    key_gain,
    queries,
    text_image,
    text_hidden,
    out_weight,
    attn_gate,
):
    groups, nblk, cores = (lax.axis_size(a) for a in ("groups", "blk", "heads"))
    lines = nblk // 2
    tok = image_feats.shape[0]
    depth = key_weight.shape[0]
    kv_cols = key_weight.shape[1]
    mine_cols = kv_cols // 2
    text_rows = queries.shape[0]
    q_half = queries.shape[1] // 2
    per_kv = q_half // mine_cols
    grp, blk, core = (lax.axis_index(a) for a in ("groups", "blk", "heads"))
    par = grp % 2
    y = blk % 2
    line = blk // 2

    swap_y = [(b, b ^ 1) for b in range(nblk)]
    swap_core = [(c, c ^ 1) for c in range(cores)]
    half = depth // 2
    fast = lines == 4 and cores == 2 and kv_cols == 2 * HD

    def along(name, array, d, ok=lambda l: True):
        with jax.named_scope(f"{name}_z{d}"):
            return lax.ppermute(array, "blk", [(b, b ^ (2 * d)) for b in range(nblk) if ok(b // 2)])

    def over_y(name, array):
        with jax.named_scope(name + "_y"):
            return lax.ppermute(array, "blk", swap_y)

    def over_core(name, array):
        with jax.named_scope(name + "_core"):
            return lax.ppermute(array, "heads", swap_core)

    def over_x(name, array):
        with jax.named_scope(name + "_x"):
            return lax.ppermute(array, "groups", [(g, g ^ 1) for g in range(groups)])

    def over_both(name, array):
        pairs = [(g * nblk + b, (g ^ 1) * nblk + (b ^ 1)) for g in range(groups) for b in range(nblk)]
        with jax.named_scope(name + "_xy"):
            return lax.ppermute(array, ("groups", "blk"), pairs)

    def hold(*arrays):
        return lax.optimization_barrier(arrays)

    def take_y(array, size, which):
        return lax.dynamic_slice_in_dim(array, which * size, size, 1)

    def middle(l):
        return l in (1, 2)

    half_lines = lines // 2

    def share(to_x, to_y):
        return jnp.concatenate(
            [
                lax.dynamic_slice_in_dim(
                    image_feats, ((2 * (core * half_lines + l) + to_y) * 2 + to_x) * half, half, 1
                )
                for l in range(half_lines)
            ],
            1,
        )

    half_lines = lines // 2
    scalars = pl.BlockSpec(memory_space=pltpu.SMEM)
    share = jax.ShapeDtypeStruct((tok, half_lines * half), BF16)

    def shares(flips, *weights):
        out_shape = [share] * len(flips) + [jax.ShapeDtypeStruct((half, kv_cols), BF16)] * len(weights)
        return pl.pallas_call(
            functools.partial(share_kernel, flips, half_lines),
            out_shape=tuple(out_shape),
            in_specs=[FREE] + [FREE] * len(weights),
            out_specs=(WHOLE,) * len(out_shape),
            scratch_shapes=[pltpu.SemaphoreType.DMA((2 + len(flips) * half_lines,))],
            compiler_params=pltpu.CompilerParams(vmem_limit_bytes=56 * 1024 * 1024),
        )(image_feats, *weights)

    share_x, share_y, key_own = shares(((1, 0), (0, 1)), key_weight)
    share_both, value_own = shares(((1, 1),), value_weight)
    q_mine, q_got = take_y(queries, q_half, y), over_y("q", take_y(queries, q_half, 1 - y))
    low_y = y == 0
    q_rows = jnp.concatenate([jnp.where(low_y, q_mine, q_got), jnp.where(low_y, q_got, q_mine)], 0)
    if fast:
        def devices(route):
            pairs = []
            for l in range(lines):
                for yy in range(2):
                    for c in range(cores):
                        to_l, to_y, to_c = route(l, yy, c)
                        pairs.append(((2 * l + yy) * cores + c, (2 * to_l + to_y) * cores + to_c))
            return pairs

        def to_head(name, tile):
            tiles = []
            for r in range(2):
                with jax.named_scope(name + "_head"):
                    tiles.append(
                        lax.ppermute(
                            tile, ("blk", "heads"), devices(lambda l, yy, c: (2 * c + yy, (l % 2) ^ r, l // 2))
                        )
                    )
            return tiles + [over_core(name + "_tile", t) for t in tiles]

        k1, km = along("wk", key_own, 1), along("wk", key_own, 3, middle)
        img_y, img_x = over_y("image", share_y), over_x("image", share_x)
        kb, ka = along("wk_across", k1, 3, middle), along("wk_out", km, 1, middle)
        kb, ka, img_y, img_x, share_both, value_own, q_rows = hold(kb, ka, img_y, img_x, share_both, value_own, q_rows)
        img_both = over_both("image", share_both)
        ke = along("wk_end", kb, 1, middle)
        v1, vm = along("wv", value_own, 1), along("wv", value_own, 3, middle)
        core_y, core_x = over_core("image", img_y), over_core("image", img_x)
        q_1 = along("q", q_rows, 1)
        v1, vm, ke, img_both, core_y, core_x, q_1 = hold(v1, vm, ke, img_both, core_y, core_x, q_1)
        q_near = jnp.concatenate([q_rows, q_1], 0)
        q_far = along("q", q_near, 2)
        core_both = over_core("image", img_both)
        vb, va = along("wv_across", v1, 3, middle), along("wv_out", vm, 1, middle)
        pass
        key_refs, value_refs = [key_own, k1, kb, ka, km, ke], [value_own, v1, vb, va, vm]
        pair = lambda i, o: ((i, 0), (o, 0))
        sources = (pair(0, 0), pair(1, 1), pair(2, 3), pair(4, 5))
    else:
        q_pieces = [q_rows if d == 0 else along("q", q_rows, d) for d in range(lines)]
        img_y, img_x, img_both = over_y("image", share_y), over_x("image", share_x), over_both("image", share_both)
        core_y, core_x, core_both = (over_core("image", i) for i in (img_y, img_x, img_both))
        key_refs = [key_own] + [along("wk", key_own, d) for d in range(1, lines)]
        value_refs = [value_own] + [along("wv", value_own, d) for d in range(1, lines)]
        sources = tuple(((d, 0), (d, 0)) for d in range(lines))
    pieces = [img_y, core_y, img_x, core_x, img_both, core_both]
    slots = slot_image.astype(F32).reshape(tok // HD, HD)
    extra = 8 * (-(-(tok // HD) // 8))

    idx = jnp.stack([par, core, y, ((line == 1) | (line == 2)).astype(jnp.int32)] + [line ^ d for d in range(lines)])
    macs = 4 * tok * half * kv_cols

    def project(weights, extra, kind):
        out = lambda rows, dtype: jax.ShapeDtypeStruct((rows, mine_cols), dtype)
        return pl.pallas_call(
            functools.partial(project_kernel, sources, extra),
            out_shape=(out(2 * tok, F32), out(2 * tok + extra, kind), out(2 * tok, kind), out(2 * tok, kind)),
            in_specs=[scalars, WHOLE] + [FREE] * (7 + len(weights)),
            out_specs=(WHOLE,) * 4,
            scratch_shapes=[
                pltpu.VMEM((lines, 4 * tok, half), BF16),
                pltpu.VMEM((lines, half, kv_cols), BF16),
                pltpu.VMEM((4 * tok, kv_cols), F32),
                pltpu.SemaphoreType.DMA((lines, 5)),
            ],
            compiler_params=BIG,
            cost_estimate=pl.CostEstimate(
                flops=2 * macs * lines, bytes_accessed=macs * lines // 32, transcendentals=0
            ),
        )(idx, slots, image_feats, *pieces, *weights)

    rows = 2 * text_rows
    keep, to_y, to_x, to_both = project(key_refs, extra, F32)
    if fast:
        vb, keep = hold(vb, keep)
    key_parts = [over_y("key", to_y), over_x("key", to_x), over_both("key", to_both)]
    if fast:
        value_refs.append(along("wv_end", vb, 1, middle))
    slot_rows = 2 * tok // HD
    packed = pl.pallas_call(
        key_kernel,
        out_shape=jax.ShapeDtypeStruct((2 * tok + slot_rows + (-slot_rows % 16), mine_cols), BF16),
        in_specs=[WHOLE] * 6,
        out_specs=WHOLE,
        compiler_params=PARAMS,
    )(keep, *key_parts, key_gain.reshape(1, HD), slots)

    keep, to_y, to_x, to_both = project(value_refs, 0, BF16)
    if fast:
        to_y, to_x, to_both, q_far = hold(to_y, to_x, to_both, q_far)
        q_pieces = [q_near, q_far]
    value_parts = [over_y("value", to_y), over_x("value", to_x), over_both("value", to_both)]
    limits = text_image.astype(F32).reshape(lines, rows)
    limits = jnp.concatenate([lax.dynamic_slice_in_dim(limits, line ^ d, 1, 0) for d in range(lines)], 0)
    limits = limits.reshape(lines * rows, 1)
    all_rows = lines * rows * per_kv
    expo, figures = pl.pallas_call(
        functools.partial(score_kernel, lines, per_kv),
        out_shape=(
            jax.ShapeDtypeStruct((all_rows, 2 * tok), BF16),
            jax.ShapeDtypeStruct((lines * rows, HD), BF16),
        ),
        in_specs=[WHOLE] * (2 + len(q_pieces)),
        out_specs=(WHOLE, WHOLE),
        scratch_shapes=[pltpu.VMEM((per_kv * rows, HD), BF16)],
        compiler_params=PARAMS,
    )(limits, packed, *q_pieces)
    value_y, value_x, value_both = (part.astype(F32) for part in value_parts)
    values = ((keep + value_y) + (value_x + value_both)).astype(BF16)
    sums = pl.pallas_call(
        functools.partial(value_kernel, lines, per_kv),
        out_shape=(jax.ShapeDtypeStruct((rows, q_half + HD), BF16),) * lines,
        in_specs=[WHOLE] * 3,
        out_specs=(WHOLE,) * lines,
        compiler_params=PARAMS,
    )(expo, figures, values)
    sums = [sums[0]] + [along("sums", sums[d], d) for d in range(1, lines)]
    attn = pl.pallas_call(
        functools.partial(combine_kernel, lines, per_kv),
        out_shape=jax.ShapeDtypeStruct((rows, q_half), BF16),
        in_specs=[WHOLE] * lines,
        out_specs=WHOLE,
        compiler_params=PARAMS,
    )(*sums)
    mine = [attn if d == 0 else along("attn", attn, d) for d in range(lines)]
    where = [(line ^ d, y) for d in range(lines)] + [(line ^ d, 1 - y) for d in range(lines)]
    other = [over_y(f"attn{d}", m) for d, m in enumerate(mine)]

    out_rows = lines * rows
    out_cols = out_weight.shape[1]
    keep, send = pl.pallas_call(
        functools.partial(proj_kernel, 2 * lines),
        out_shape=(
            jax.ShapeDtypeStruct((out_rows // 2, out_cols), F32),
            jax.ShapeDtypeStruct((out_rows // 2, out_cols), BF16),
        ),
        in_specs=[scalars] + [WHOLE] * (2 * lines + 1),
        out_specs=(WHOLE, WHOLE),
        scratch_shapes=[pltpu.VMEM((out_rows, 2 * q_half), BF16), pltpu.VMEM((out_rows, out_cols), F32)],
        compiler_params=PARAMS,
    )(jnp.stack([core] + [i for pair in where for i in pair]), *mine, *other, out_weight)
    head_total = keep + over_core("proj", send).astype(F32)
    return (text_hidden.astype(F32) + jnp.tanh(attn_gate[0]) * head_total).astype(BF16)


def solution(mesh):
    placed = (
        P(("groups", "blk"), None),
        P(("groups", "blk")),
        P("blk", "heads"),
        P("blk", "heads"),
        P(),
        P(("groups", "blk"), "heads"),
        P("groups"),
        P(("groups", "heads"), "blk"),
        P("heads", "blk"),
        P(),
    )
    return jax.shard_map(
        body, mesh=mesh, in_specs=placed, out_specs=P(("groups", "heads"), "blk"), check_vma=False
    )
```

```python
import functools
import math

import jax
import jax.numpy as jnp
from jax import lax
from jax.experimental import pallas as pl
from jax.experimental.pallas import tpu as pltpu
from jax.sharding import PartitionSpec as P

HD = 128
F32 = jnp.float32
BF16 = jnp.bfloat16
VMEM_BYTES = 20 * 1024 * 1024
PARAMS = pltpu.CompilerParams(vmem_limit_bytes=VMEM_BYTES)
BIG = pltpu.CompilerParams(vmem_limit_bytes=52 * 1024 * 1024)
WHOLE = pl.BlockSpec(memory_space=pltpu.VMEM)
FREE = pl.BlockSpec(memory_space=pltpu.HBM)


def dot(a, b):
    return jnp.dot(a, b, preferred_element_type=F32)


def dot_nt(a, b):
    return lax.dot_general(a, b, (((1,), (1,)), ((), ())), preferred_element_type=F32)


def share_kernel(flips, half_lines, image, *refs):
    par, core, y = lax.axis_index("groups") % 2, lax.axis_index("heads"), lax.axis_index("blk") % 2
    n = len(flips)
    n_weights = (len(refs) - n - 1) // 2
    weights, outs, sems = refs[:n_weights], refs[n_weights:-1], refs[-1]
    copies = []
    for weight, own in zip(weights, outs[n:]):
        half = own.shape[0]
        copies.append((weight.at[pl.ds(pl.multiple_of(par * half, half), half), :], own))
    for (flip_x, flip_y), out in zip(flips, outs):
        half = out.shape[1] // half_lines
        to_par = 1 - par if flip_x else par
        to_y = 1 - y if flip_y else y
        for l in range(half_lines):
            at = pl.multiple_of(((2 * (core * half_lines + l) + to_y) * 2 + to_par) * half, half)
            copies.append((image.at[:, pl.ds(at, half)], out.at[:, pl.ds(l * half, half)]))
    copies = [pltpu.make_async_copy(src, dst, sems.at[i]) for i, (src, dst) in enumerate(copies)]
    for c in copies:
        c.start()
    for c in copies:
        c.wait()


def load_shards(first, sources, idx_ref, image, got, weights, x_ref, w_ref, sems):
    par, core, y, inner = idx_ref[0], idx_ref[1], idx_ref[2], idx_ref[3]
    rows = image.shape[0]
    half = x_ref.shape[2]
    half_lines = got[0].shape[1] // half
    cols = weights[0].shape[1]

    def copy(src, dst, k, i):
        return pltpu.make_async_copy(src, dst, sems.at[k, i])

    waits = []
    for k, projections in enumerate(sources):
        line = idx_ref[4 + first + k]
        own_at = pl.multiple_of(((2 * line + y) * 2 + par) * half, half)
        here = line // half_lines == core
        got_at = pl.multiple_of(lax.rem(line, half_lines) * half, half)
        own = copy(image.at[:, pl.ds(own_at, half)], x_ref.at[k, pl.ds(0, rows), :], k, 0)
        own.start()

        def from_core(which, k=k, got_at=got_at):
            return [
                copy(
                    got[2 * i + which].at[:, pl.ds(got_at, half)],
                    x_ref.at[k, pl.ds((i + 1) * rows, rows), :],
                    k,
                    1 + i,
                )
                for i in range(3)
            ]

        mine = from_core(0)

        @pl.when(here)
        def _(mine=mine):
            for c in mine:
                c.start()

        @pl.when(jnp.logical_not(here))
        def _(from_core=from_core):
            for c in from_core(1):
                c.start()

        waits.append([own] + mine)
        for p, (in_src, out_src) in enumerate(projections):

            def from_weight(src, k=k, p=p):
                return copy(
                    weights[src[0]].at[pl.ds(src[1], half), :], w_ref.at[k, :, pl.ds(p * cols, cols)], k, 4 + p
                )

            weight = from_weight(in_src)
            if in_src == out_src:
                weight.start()
            else:

                @pl.when(inner > 0)
                def _(weight=weight):
                    weight.start()

                @pl.when(inner <= 0)
                def _(from_weight=from_weight, out_src=out_src):
                    from_weight(out_src).start()

            waits[-1].append(weight)
    return waits


def project_kernel(sources, extra, idx_ref, slots, image, *refs):
    got, weights = refs[:6], refs[6:-8]
    (keep, to_y, to_x, to_both), (x_ref, w_ref, acc_ref, sems) = refs[-8:-4], refs[-4:]
    y = idx_ref[2]
    rows = image.shape[0]
    cols = keep.shape[1]
    kind = to_y.dtype
    waits = load_shards(0, tuple((s,) for s in sources), idx_ref, image, got, weights, x_ref, w_ref, sems)
    for k, copies in enumerate(waits):
        for c in copies:
            c.wait()
        part = dot(x_ref[k], w_ref[k])
        if k == 0:
            acc_ref[...] = part
        elif k < len(waits) - 1:
            acc_ref[...] += part
    total = acc_ref[...] + part
    low = y == 0
    mine = jnp.where(low, total[:, :cols], total[:, cols:])
    other = jnp.where(low, total[:, cols:], total[:, :cols]).astype(kind)
    keep[...] = mine[: 2 * rows]
    to_y[:rows, :] = other[rows : 2 * rows]
    to_y[rows : 2 * rows, :] = other[:rows]
    to_x[...] = mine[2 * rows :].astype(kind)
    to_both[:rows, :] = other[3 * rows :]
    to_both[rows:, :] = other[2 * rows : 3 * rows]
    if extra:
        n = slots.shape[0]
        to_y[2 * rows : 2 * rows + n, :HD] = slots[...]
        to_y[2 * rows + n :, :] = jnp.zeros((extra - n, cols), kind)
        if cols > HD:
            to_y[2 * rows : 2 * rows + n, HD:] = jnp.zeros((n, cols - HD), kind)


def key_kernel(keep, got_y, got_x, got_both, gain, slots, out):
    rows = keep.shape[0]
    n = slots.shape[0]
    raw = (keep[...] + got_y[:rows, :]) + (got_x[...] + got_both[...])
    for c in range(0, raw.shape[1], HD):
        part = raw[:, c : c + HD]
        scale = lax.rsqrt(jnp.mean(part * part, axis=-1, keepdims=True) + 1e-05)
        out[:rows, c : c + HD] = (part * scale * gain[...]).astype(BF16)
    pad = jnp.zeros((out.shape[0] - rows - 2 * n, HD), F32)
    out[rows:, :HD] = jnp.concatenate([slots[...], got_y[rows : rows + n, :HD], pad], 0).astype(BF16)


def score_kernel(n, heads, limit_ref, keys_ref, *refs):
    *queries, expo_ref, figures_ref, q_ref = refs
    rows = limit_ref.shape[0] // n
    each = n // len(queries)
    tokens = expo_ref.shape[1]
    scale = 1.0 / math.sqrt(HD)
    slots = keys_ref[tokens : tokens + 16 * (-(-tokens // HD) // 16 + (-(-tokens // HD) % 16 > 0)), :].astype(F32)
    lane = lax.broadcasted_iota(jnp.int32, (rows, HD), 1)
    for i in range(n):
        limit = limit_ref[i * rows : (i + 1) * rows, :]
        seen = []
        for c in range(tokens // HD):
            slot = slots[c : c + 1, :]
            seen.append(jnp.where((slot >= 0.0) & (slot <= limit), 1.0, 0.0))
        seen = jnp.concatenate(seen, 1)
        for j in range(heads):
            at = i % each * rows
            q_ref[j * rows : (j + 1) * rows, :] = queries[i // each][at : at + rows, j * HD : (j + 1) * HD]
        s = dot_nt(q_ref[...], keys_ref[:tokens, :]) * scale
        s = jnp.where(seen[None] > 0.5, s.reshape(heads, rows, tokens), -1e30).reshape(heads * rows, tokens)
        top = jnp.max(s, axis=1, keepdims=True).astype(BF16).astype(F32)
        e = jnp.where(s > -1e29, jnp.exp(s - top), 0.0)
        total = jnp.sum(e, axis=1, keepdims=True)
        expo_ref[i * heads * rows : (i + 1) * heads * rows, :] = e.astype(BF16)
        high = total.astype(BF16).astype(F32)
        figures = jnp.zeros((rows, HD), F32)
        for j in range(heads):
            part = slice(j * rows, (j + 1) * rows)
            figures = jnp.where(lane == j, top[part], figures)
            figures = jnp.where(lane == heads + j, high[part], figures)
            figures = jnp.where(lane == 2 * heads + j, total[part] - high[part], figures)
        figures_ref[i * rows : (i + 1) * rows, :] = figures.astype(BF16)


def value_kernel(n, heads, expo_ref, figures_ref, values_ref, *outs):
    rows = figures_ref.shape[0] // n
    for i in range(n):
        acc = dot(expo_ref[i * heads * rows : (i + 1) * heads * rows, :], values_ref[...]).astype(BF16)
        for j in range(heads):
            outs[i][:, j * HD : (j + 1) * HD] = acc[j * rows : (j + 1) * rows, :]
        outs[i][:, heads * HD :] = figures_ref[i * rows : (i + 1) * rows, :]


def combine_kernel(n, heads, *refs):
    parts, out_ref = refs[:n], refs[n]
    rows = out_ref.shape[0]
    lane = lax.broadcasted_iota(jnp.int32, (rows, HD), 1)
    figures = [part[:, heads * HD :].astype(F32) for part in parts]

    def column(figure, at):
        return jnp.sum(jnp.where(lane == at, figure, 0.0), axis=1, keepdims=True)

    for j in range(heads):
        tops = [column(f, j) for f in figures]
        top = functools.reduce(jnp.maximum, tops)
        total = jnp.zeros((rows, 1), F32)
        acc = jnp.zeros((rows, HD), F32)
        for part, figure, own_top in zip(parts, figures, tops):
            weight = jnp.exp(own_top - top)
            total = total + weight * (column(figure, heads + j) + column(figure, 2 * heads + j))
            acc = acc + weight * part[:, j * HD : (j + 1) * HD].astype(F32)
        out_ref[:, j * HD : (j + 1) * HD] = (acc / total).astype(BF16)


def proj_kernel(n, idx_ref, *refs):
    pieces = refs[:n]
    w_ref, keep_ref, send_ref, a_ref, p_ref = refs[n:]
    rows, width = pieces[0].shape
    for k in range(n):
        at_row = pl.multiple_of(idx_ref[1 + 2 * k] * rows, rows)
        at_col = pl.multiple_of(idx_ref[2 + 2 * k] * width, width)
        a_ref[pl.ds(at_row, rows), pl.ds(at_col, width)] = pieces[k][...]
    p_ref[...] = dot(a_ref[...], w_ref[...])
    size = keep_ref.shape[0]
    core = idx_ref[0]
    keep_ref[...] = p_ref[pl.ds(pl.multiple_of(core * size, size), size), :]
    send_ref[...] = p_ref[pl.ds(pl.multiple_of((1 - core) * size, size), size), :].astype(BF16)


def body(
    image_feats,
    slot_image,
    key_weight,
    value_weight,
    key_gain,
    queries,
    text_image,
    text_hidden,
    out_weight,
    attn_gate,
):
    groups, nblk, cores = (lax.axis_size(a) for a in ("groups", "blk", "heads"))
    lines = nblk // 2
    tok = image_feats.shape[0]
    depth = key_weight.shape[0]
    kv_cols = key_weight.shape[1]
    mine_cols = kv_cols // 2
    text_rows = queries.shape[0]
    q_half = queries.shape[1] // 2
    per_kv = q_half // mine_cols
    grp, blk, core = (lax.axis_index(a) for a in ("groups", "blk", "heads"))
    par = grp % 2
    y = blk % 2
    line = blk // 2

    swap_y = [(b, b ^ 1) for b in range(nblk)]
    swap_core = [(c, c ^ 1) for c in range(cores)]
    half = depth // 2
    fast = lines == 4 and cores == 2 and kv_cols == 2 * HD

    def along(name, array, d, ok=lambda l: True):
        with jax.named_scope(f"{name}_z{d}"):
            return lax.ppermute(array, "blk", [(b, b ^ (2 * d)) for b in range(nblk) if ok(b // 2)])

    def over_y(name, array):
        with jax.named_scope(name + "_y"):
            return lax.ppermute(array, "blk", swap_y)

    def over_core(name, array):
        with jax.named_scope(name + "_core"):
            return lax.ppermute(array, "heads", swap_core)

    def over_x(name, array):
        with jax.named_scope(name + "_x"):
            return lax.ppermute(array, "groups", [(g, g ^ 1) for g in range(groups)])

    def over_both(name, array):
        pairs = [(g * nblk + b, (g ^ 1) * nblk + (b ^ 1)) for g in range(groups) for b in range(nblk)]
        with jax.named_scope(name + "_xy"):
            return lax.ppermute(array, ("groups", "blk"), pairs)

    def hold(*arrays):
        return lax.optimization_barrier(arrays)

    def take_y(array, size, which):
        return lax.dynamic_slice_in_dim(array, which * size, size, 1)

    def middle(l):
        return l in (1, 2)

    half_lines = lines // 2

    def share(to_x, to_y):
        return jnp.concatenate(
            [
                lax.dynamic_slice_in_dim(
                    image_feats, ((2 * (core * half_lines + l) + to_y) * 2 + to_x) * half, half, 1
                )
                for l in range(half_lines)
            ],
            1,
        )

    half_lines = lines // 2
    scalars = pl.BlockSpec(memory_space=pltpu.SMEM)
    share = jax.ShapeDtypeStruct((tok, half_lines * half), BF16)

    def shares(flips, *weights):
        out_shape = [share] * len(flips) + [jax.ShapeDtypeStruct((half, kv_cols), BF16)] * len(weights)
        return pl.pallas_call(
            functools.partial(share_kernel, flips, half_lines),
            out_shape=tuple(out_shape),
            in_specs=[FREE] + [FREE] * len(weights),
            out_specs=(WHOLE,) * len(out_shape),
            scratch_shapes=[pltpu.SemaphoreType.DMA((2 + len(flips) * half_lines,))],
            compiler_params=pltpu.CompilerParams(vmem_limit_bytes=56 * 1024 * 1024),
        )(image_feats, *weights)

    share_x, share_y, key_own = shares(((1, 0), (0, 1)), key_weight)
    share_both, value_own = shares(((1, 1),), value_weight)
    q_mine, q_got = take_y(queries, q_half, y), over_y("q", take_y(queries, q_half, 1 - y))
    low_y = y == 0
    q_rows = jnp.concatenate([jnp.where(low_y, q_mine, q_got), jnp.where(low_y, q_got, q_mine)], 0)
    if fast:
        def devices(route):
            pairs = []
            for l in range(lines):
                for yy in range(2):
                    for c in range(cores):
                        to_l, to_y, to_c = route(l, yy, c)
                        pairs.append(((2 * l + yy) * cores + c, (2 * to_l + to_y) * cores + to_c))
            return pairs

        def to_head(name, tile):
            tiles = []
            for r in range(2):
                with jax.named_scope(name + "_head"):
                    tiles.append(
                        lax.ppermute(
                            tile, ("blk", "heads"), devices(lambda l, yy, c: (2 * c + yy, (l % 2) ^ r, l // 2))
                        )
                    )
            return tiles + [over_core(name + "_tile", t) for t in tiles]

        k1, km = along("wk", key_own, 1), along("wk", key_own, 3, middle)
        img_y, img_x = over_y("image", share_y), over_x("image", share_x)
        kb, ka = along("wk_across", k1, 3, middle), along("wk_out", km, 1, middle)
        kb, ka, img_y, img_x, share_both, value_own, q_rows = hold(kb, ka, img_y, img_x, share_both, value_own, q_rows)
        img_both = over_both("image", share_both)
        ke = along("wk_end", kb, 1, middle)
        v1, vm = along("wv", value_own, 1), along("wv", value_own, 3, middle)
        core_y, core_x = over_core("image", img_y), over_core("image", img_x)
        v1, vm, ke, img_both, core_y, core_x = hold(v1, vm, ke, img_both, core_y, core_x)
        q_1 = along("q", q_rows, 1)
        core_both = over_core("image", img_both)
        vb, va = along("wv_across", v1, 3, middle), along("wv_out", vm, 1, middle)
        pass
        key_refs, value_refs = [key_own, k1, kb, ka, km, ke], [value_own, v1, vb, va, vm]
        pair = lambda i, o: ((i, 0), (o, 0))
        sources = (pair(0, 0), pair(1, 1), pair(2, 3), pair(4, 5))
    else:
        q_pieces = [q_rows if d == 0 else along("q", q_rows, d) for d in range(lines)]
        img_y, img_x, img_both = over_y("image", share_y), over_x("image", share_x), over_both("image", share_both)
        core_y, core_x, core_both = (over_core("image", i) for i in (img_y, img_x, img_both))
        key_refs = [key_own] + [along("wk", key_own, d) for d in range(1, lines)]
        value_refs = [value_own] + [along("wv", value_own, d) for d in range(1, lines)]
        sources = tuple(((d, 0), (d, 0)) for d in range(lines))
    pieces = [img_y, core_y, img_x, core_x, img_both, core_both]
    slots = slot_image.astype(F32).reshape(tok // HD, HD)
    extra = 8 * (-(-(tok // HD) // 8))

    idx = jnp.stack([par, core, y, ((line == 1) | (line == 2)).astype(jnp.int32)] + [line ^ d for d in range(lines)])
    macs = 4 * tok * half * kv_cols

    def project(weights, extra, kind):
        out = lambda rows, dtype: jax.ShapeDtypeStruct((rows, mine_cols), dtype)
        return pl.pallas_call(
            functools.partial(project_kernel, sources, extra),
            out_shape=(out(2 * tok, F32), out(2 * tok + extra, kind), out(2 * tok, kind), out(2 * tok, kind)),
            in_specs=[scalars, WHOLE] + [FREE] * (7 + len(weights)),
            out_specs=(WHOLE,) * 4,
            scratch_shapes=[
                pltpu.VMEM((lines, 4 * tok, half), BF16),
                pltpu.VMEM((lines, half, kv_cols), BF16),
                pltpu.VMEM((4 * tok, kv_cols), F32),
                pltpu.SemaphoreType.DMA((lines, 5)),
            ],
            compiler_params=BIG,
            cost_estimate=pl.CostEstimate(
                flops=2 * macs * lines, bytes_accessed=macs * lines // 32, transcendentals=0
            ),
        )(idx, slots, image_feats, *pieces, *weights)

    rows = 2 * text_rows
    keep, to_y, to_x, to_both = project(key_refs, extra, F32)
    if fast:
        vb, keep, q_1 = hold(vb, keep, q_1)
        q_near = jnp.concatenate([q_rows, q_1], 0)
        q_far = along("q", q_near, 2)
    key_parts = [over_y("key", to_y), over_x("key", to_x), over_both("key", to_both)]
    if fast:
        value_refs.append(along("wv_end", vb, 1, middle))
    slot_rows = 2 * tok // HD
    packed = pl.pallas_call(
        key_kernel,
        out_shape=jax.ShapeDtypeStruct((2 * tok + slot_rows + (-slot_rows % 16), mine_cols), BF16),
        in_specs=[WHOLE] * 6,
        out_specs=WHOLE,
        compiler_params=PARAMS,
    )(keep, *key_parts, key_gain.reshape(1, HD), slots)

    keep, to_y, to_x, to_both = project(value_refs, 0, BF16)
    if fast:
        to_y, to_x, to_both, q_far = hold(to_y, to_x, to_both, q_far)
        q_pieces = [q_near, q_far]
    value_parts = [over_y("value", to_y), over_x("value", to_x), over_both("value", to_both)]
    limits = text_image.astype(F32).reshape(lines, rows)
    limits = jnp.concatenate([lax.dynamic_slice_in_dim(limits, line ^ d, 1, 0) for d in range(lines)], 0)
    limits = limits.reshape(lines * rows, 1)
    all_rows = lines * rows * per_kv
    expo, figures = pl.pallas_call(
        functools.partial(score_kernel, lines, per_kv),
        out_shape=(
            jax.ShapeDtypeStruct((all_rows, 2 * tok), BF16),
            jax.ShapeDtypeStruct((lines * rows, HD), BF16),
        ),
        in_specs=[WHOLE] * (2 + len(q_pieces)),
        out_specs=(WHOLE, WHOLE),
        scratch_shapes=[pltpu.VMEM((per_kv * rows, HD), BF16)],
        compiler_params=PARAMS,
    )(limits, packed, *q_pieces)
    value_y, value_x, value_both = (part.astype(F32) for part in value_parts)
    values = ((keep + value_y) + (value_x + value_both)).astype(BF16)
    sums = pl.pallas_call(
        functools.partial(value_kernel, lines, per_kv),
        out_shape=(jax.ShapeDtypeStruct((rows, q_half + HD), BF16),) * lines,
        in_specs=[WHOLE] * 3,
        out_specs=(WHOLE,) * lines,
        compiler_params=PARAMS,
    )(expo, figures, values)
    sums = [sums[0]] + [along("sums", sums[d], d) for d in range(1, lines)]
    attn = pl.pallas_call(
        functools.partial(combine_kernel, lines, per_kv),
        out_shape=jax.ShapeDtypeStruct((rows, q_half), BF16),
        in_specs=[WHOLE] * lines,
        out_specs=WHOLE,
        compiler_params=PARAMS,
    )(*sums)
    mine = [attn if d == 0 else along("attn", attn, d) for d in range(lines)]
    where = [(line ^ d, y) for d in range(lines)] + [(line ^ d, 1 - y) for d in range(lines)]
    other = [over_y(f"attn{d}", m) for d, m in enumerate(mine)]

    out_rows = lines * rows
    out_cols = out_weight.shape[1]
    keep, send = pl.pallas_call(
        functools.partial(proj_kernel, 2 * lines),
        out_shape=(
            jax.ShapeDtypeStruct((out_rows // 2, out_cols), F32),
            jax.ShapeDtypeStruct((out_rows // 2, out_cols), BF16),
        ),
        in_specs=[scalars] + [WHOLE] * (2 * lines + 1),
        out_specs=(WHOLE, WHOLE),
        scratch_shapes=[pltpu.VMEM((out_rows, 2 * q_half), BF16), pltpu.VMEM((out_rows, out_cols), F32)],
        compiler_params=PARAMS,
    )(jnp.stack([core] + [i for pair in where for i in pair]), *mine, *other, out_weight)
    head_total = keep + over_core("proj", send).astype(F32)
    return (text_hidden.astype(F32) + jnp.tanh(attn_gate[0]) * head_total).astype(BF16)


def solution(mesh):
    placed = (
        P(("groups", "blk"), None),
        P(("groups", "blk")),
        P("blk", "heads"),
        P("blk", "heads"),
        P(),
        P(("groups", "blk"), "heads"),
        P("groups"),
        P(("groups", "heads"), "blk"),
        P("heads", "blk"),
        P(),
    )
    return jax.shard_map(
        body, mesh=mesh, in_specs=placed, out_specs=P(("groups", "heads"), "blk"), check_vma=False
    )
```

```python
import functools
import math

import jax
import jax.numpy as jnp
from jax import lax
from jax.experimental import pallas as pl
from jax.experimental.pallas import tpu as pltpu
from jax.sharding import PartitionSpec as P

HD = 128
F32 = jnp.float32
BF16 = jnp.bfloat16
VMEM_BYTES = 20 * 1024 * 1024
PARAMS = pltpu.CompilerParams(vmem_limit_bytes=VMEM_BYTES)
BIG = pltpu.CompilerParams(vmem_limit_bytes=52 * 1024 * 1024)
WHOLE = pl.BlockSpec(memory_space=pltpu.VMEM)
FREE = pl.BlockSpec(memory_space=pltpu.HBM)


def dot(a, b):
    return jnp.dot(a, b, preferred_element_type=F32)


def dot_nt(a, b):
    return lax.dot_general(a, b, (((1,), (1,)), ((), ())), preferred_element_type=F32)


def share_kernel(flips, half_lines, image, *refs):
    par, core, y = lax.axis_index("groups") % 2, lax.axis_index("heads"), lax.axis_index("blk") % 2
    n = len(flips)
    n_weights = (len(refs) - n - 1) // 2
    weights, outs, sems = refs[:n_weights], refs[n_weights:-1], refs[-1]
    copies = []
    for weight, own in zip(weights, outs[n:]):
        half = own.shape[0]
        copies.append((weight.at[pl.ds(pl.multiple_of(par * half, half), half), :], own))
    for (flip_x, flip_y), out in zip(flips, outs):
        half = out.shape[1] // half_lines
        to_par = 1 - par if flip_x else par
        to_y = 1 - y if flip_y else y
        for l in range(half_lines):
            at = pl.multiple_of(((2 * (core * half_lines + l) + to_y) * 2 + to_par) * half, half)
            copies.append((image.at[:, pl.ds(at, half)], out.at[:, pl.ds(l * half, half)]))
    copies = [pltpu.make_async_copy(src, dst, sems.at[i]) for i, (src, dst) in enumerate(copies)]
    for c in copies:
        c.start()
    for c in copies:
        c.wait()


def load_shards(first, sources, idx_ref, image, got, weights, x_ref, w_ref, sems):
    par, core, y, inner = idx_ref[0], idx_ref[1], idx_ref[2], idx_ref[3]
    rows = image.shape[0]
    half = x_ref.shape[2]
    half_lines = got[0].shape[1] // half
    cols = weights[0].shape[1]

    def copy(src, dst, k, i):
        return pltpu.make_async_copy(src, dst, sems.at[k, i])

    waits = []
    for k, projections in enumerate(sources):
        line = idx_ref[4 + first + k]
        own_at = pl.multiple_of(((2 * line + y) * 2 + par) * half, half)
        here = line // half_lines == core
        got_at = pl.multiple_of(lax.rem(line, half_lines) * half, half)
        own = copy(image.at[:, pl.ds(own_at, half)], x_ref.at[k, pl.ds(0, rows), :], k, 0)
        own.start()

        def from_core(which, k=k, got_at=got_at):
            return [
                copy(
                    got[2 * i + which].at[:, pl.ds(got_at, half)],
                    x_ref.at[k, pl.ds((i + 1) * rows, rows), :],
                    k,
                    1 + i,
                )
                for i in range(3)
            ]

        mine = from_core(0)

        @pl.when(here)
        def _(mine=mine):
            for c in mine:
                c.start()

        @pl.when(jnp.logical_not(here))
        def _(from_core=from_core):
            for c in from_core(1):
                c.start()

        waits.append([own] + mine)
        for p, (in_src, out_src) in enumerate(projections):

            def from_weight(src, k=k, p=p):
                return copy(
                    weights[src[0]].at[pl.ds(src[1], half), :], w_ref.at[k, :, pl.ds(p * cols, cols)], k, 4 + p
                )

            weight = from_weight(in_src)
            if in_src == out_src:
                weight.start()
            else:

                @pl.when(inner > 0)
                def _(weight=weight):
                    weight.start()

                @pl.when(inner <= 0)
                def _(from_weight=from_weight, out_src=out_src):
                    from_weight(out_src).start()

            waits[-1].append(weight)
    return waits


def project_kernel(sources, extra, idx_ref, slots, image, *refs):
    got, weights = refs[:6], refs[6:-8]
    (keep, to_y, to_x, to_both), (x_ref, w_ref, acc_ref, sems) = refs[-8:-4], refs[-4:]
    y = idx_ref[2]
    rows = image.shape[0]
    cols = keep.shape[1]
    kind = to_y.dtype
    waits = load_shards(0, tuple((s,) for s in sources), idx_ref, image, got, weights, x_ref, w_ref, sems)
    for k, copies in enumerate(waits):
        for c in copies:
            c.wait()
        part = dot(x_ref[k], w_ref[k])
        if k == 0:
            acc_ref[...] = part
        elif k < len(waits) - 1:
            acc_ref[...] += part
    total = acc_ref[...] + part
    low = y == 0
    mine = jnp.where(low, total[:, :cols], total[:, cols:])
    other = jnp.where(low, total[:, cols:], total[:, :cols]).astype(kind)
    keep[...] = mine[: 2 * rows]
    to_y[:rows, :] = other[rows : 2 * rows]
    to_y[rows : 2 * rows, :] = other[:rows]
    to_x[...] = mine[2 * rows :].astype(kind)
    to_both[:rows, :] = other[3 * rows :]
    to_both[rows:, :] = other[2 * rows : 3 * rows]
    if extra:
        n = slots.shape[0]
        to_y[2 * rows : 2 * rows + n, :HD] = slots[...]
        to_y[2 * rows + n :, :] = jnp.zeros((extra - n, cols), kind)
        if cols > HD:
            to_y[2 * rows : 2 * rows + n, HD:] = jnp.zeros((n, cols - HD), kind)


def key_kernel(keep, got_y, got_x, got_both, gain, slots, out):
    rows = keep.shape[0]
    n = slots.shape[0]
    raw = (keep[...] + got_y[:rows, :]) + (got_x[...] + got_both[...])
    for c in range(0, raw.shape[1], HD):
        part = raw[:, c : c + HD]
        scale = lax.rsqrt(jnp.mean(part * part, axis=-1, keepdims=True) + 1e-05)
        out[:rows, c : c + HD] = (part * scale * gain[...]).astype(BF16)
    pad = jnp.zeros((out.shape[0] - rows - 2 * n, HD), F32)
    out[rows:, :HD] = jnp.concatenate([slots[...], got_y[rows : rows + n, :HD], pad], 0).astype(BF16)


def score_kernel(n, heads, limit_ref, keys_ref, *refs):
    *queries, expo_ref, figures_ref, q_ref = refs
    rows = limit_ref.shape[0] // n
    each = n // len(queries)
    tokens = expo_ref.shape[1]
    scale = 1.0 / math.sqrt(HD)
    slots = keys_ref[tokens : tokens + 16 * (-(-tokens // HD) // 16 + (-(-tokens // HD) % 16 > 0)), :].astype(F32)
    lane = lax.broadcasted_iota(jnp.int32, (rows, HD), 1)
    for i in range(n):
        limit = limit_ref[i * rows : (i + 1) * rows, :]
        seen = []
        for c in range(tokens // HD):
            slot = slots[c : c + 1, :]
            seen.append(jnp.where((slot >= 0.0) & (slot <= limit), 1.0, 0.0))
        seen = jnp.concatenate(seen, 1)
        for j in range(heads):
            at = i % each * rows
            q_ref[j * rows : (j + 1) * rows, :] = queries[i // each][at : at + rows, j * HD : (j + 1) * HD]
        s = dot_nt(q_ref[...], keys_ref[:tokens, :]) * scale
        s = jnp.where(seen[None] > 0.5, s.reshape(heads, rows, tokens), -1e30).reshape(heads * rows, tokens)
        top = jnp.max(s, axis=1, keepdims=True).astype(BF16).astype(F32)
        e = jnp.where(s > -1e29, jnp.exp(s - top), 0.0)
        total = jnp.sum(e, axis=1, keepdims=True)
        expo_ref[i * heads * rows : (i + 1) * heads * rows, :] = e.astype(BF16)
        high = total.astype(BF16).astype(F32)
        figures = jnp.zeros((rows, HD), F32)
        for j in range(heads):
            part = slice(j * rows, (j + 1) * rows)
            figures = jnp.where(lane == j, top[part], figures)
            figures = jnp.where(lane == heads + j, high[part], figures)
            figures = jnp.where(lane == 2 * heads + j, total[part] - high[part], figures)
        figures_ref[i * rows : (i + 1) * rows, :] = figures.astype(BF16)


def value_kernel(n, heads, expo_ref, figures_ref, keep, got_y, got_x, got_both, *outs):
    rows = figures_ref.shape[0] // n
    values = ((keep[...] + got_y[...].astype(F32)) + (got_x[...].astype(F32) + got_both[...].astype(F32))).astype(BF16)
    for i in range(n):
        acc = dot(expo_ref[i * heads * rows : (i + 1) * heads * rows, :], values).astype(BF16)
        for j in range(heads):
            outs[i][:, j * HD : (j + 1) * HD] = acc[j * rows : (j + 1) * rows, :]
        outs[i][:, heads * HD :] = figures_ref[i * rows : (i + 1) * rows, :]


def combine_kernel(n, heads, *refs):
    parts, out_ref = refs[:n], refs[n]
    rows = out_ref.shape[0]
    lane = lax.broadcasted_iota(jnp.int32, (rows, HD), 1)
    figures = [part[:, heads * HD :].astype(F32) for part in parts]

    def column(figure, at):
        return jnp.sum(jnp.where(lane == at, figure, 0.0), axis=1, keepdims=True)

    for j in range(heads):
        tops = [column(f, j) for f in figures]
        top = functools.reduce(jnp.maximum, tops)
        total = jnp.zeros((rows, 1), F32)
        acc = jnp.zeros((rows, HD), F32)
        for part, figure, own_top in zip(parts, figures, tops):
            weight = jnp.exp(own_top - top)
            total = total + weight * (column(figure, heads + j) + column(figure, 2 * heads + j))
            acc = acc + weight * part[:, j * HD : (j + 1) * HD].astype(F32)
        out_ref[:, j * HD : (j + 1) * HD] = (acc / total).astype(BF16)


def proj_kernel(n, idx_ref, *refs):
    pieces = refs[:n]
    far_ref, keep_ref, send_ref, a_ref, p_ref, w_ref, sems = refs[n:]
    rows, width = pieces[0].shape
    steps, depth = w_ref.shape[:2]
    copies = [
        pltpu.make_async_copy(far_ref.at[pl.ds(i * depth, depth), :], w_ref.at[i], sems.at[i]) for i in range(steps)
    ]
    for c in copies:
        c.start()
    for k in range(n):
        at_row = pl.multiple_of(idx_ref[1 + 2 * k] * rows, rows)
        at_col = pl.multiple_of(idx_ref[2 + 2 * k] * width, width)
        a_ref[pl.ds(at_row, rows), pl.ds(at_col, width)] = pieces[k][...]
    for i, c in enumerate(copies):
        c.wait()
        part = dot(a_ref[:, i * depth : (i + 1) * depth], w_ref[i])
        if i == 0:
            p_ref[...] = part
        else:
            p_ref[...] += part
    size = keep_ref.shape[0]
    core = idx_ref[0]
    keep_ref[...] = p_ref[pl.ds(pl.multiple_of(core * size, size), size), :]
    send_ref[...] = p_ref[pl.ds(pl.multiple_of((1 - core) * size, size), size), :].astype(BF16)


def body(
    image_feats,
    slot_image,
    key_weight,
    value_weight,
    key_gain,
    queries,
    text_image,
    text_hidden,
    out_weight,
    attn_gate,
):
    groups, nblk, cores = (lax.axis_size(a) for a in ("groups", "blk", "heads"))
    lines = nblk // 2
    tok = image_feats.shape[0]
    depth = key_weight.shape[0]
    kv_cols = key_weight.shape[1]
    mine_cols = kv_cols // 2
    text_rows = queries.shape[0]
    q_half = queries.shape[1] // 2
    per_kv = q_half // mine_cols
    grp, blk, core = (lax.axis_index(a) for a in ("groups", "blk", "heads"))
    par = grp % 2
    y = blk % 2
    line = blk // 2

    swap_y = [(b, b ^ 1) for b in range(nblk)]
    swap_core = [(c, c ^ 1) for c in range(cores)]
    half = depth // 2
    fast = lines == 4 and cores == 2 and kv_cols == 2 * HD

    def along(name, array, d, ok=lambda l: True):
        with jax.named_scope(f"{name}_z{d}"):
            return lax.ppermute(array, "blk", [(b, b ^ (2 * d)) for b in range(nblk) if ok(b // 2)])

    def over_y(name, array):
        with jax.named_scope(name + "_y"):
            return lax.ppermute(array, "blk", swap_y)

    def over_core(name, array):
        with jax.named_scope(name + "_core"):
            return lax.ppermute(array, "heads", swap_core)

    def over_x(name, array):
        with jax.named_scope(name + "_x"):
            return lax.ppermute(array, "groups", [(g, g ^ 1) for g in range(groups)])

    def over_both(name, array):
        pairs = [(g * nblk + b, (g ^ 1) * nblk + (b ^ 1)) for g in range(groups) for b in range(nblk)]
        with jax.named_scope(name + "_xy"):
            return lax.ppermute(array, ("groups", "blk"), pairs)

    def hold(*arrays):
        return lax.optimization_barrier(arrays)

    def take_y(array, size, which):
        return lax.dynamic_slice_in_dim(array, which * size, size, 1)

    def middle(l):
        return l in (1, 2)

    half_lines = lines // 2

    def share(to_x, to_y):
        return jnp.concatenate(
            [
                lax.dynamic_slice_in_dim(
                    image_feats, ((2 * (core * half_lines + l) + to_y) * 2 + to_x) * half, half, 1
                )
                for l in range(half_lines)
            ],
            1,
        )

    half_lines = lines // 2
    scalars = pl.BlockSpec(memory_space=pltpu.SMEM)
    share = jax.ShapeDtypeStruct((tok, half_lines * half), BF16)

    def shares(flips, *weights):
        out_shape = [share] * len(flips) + [jax.ShapeDtypeStruct((half, kv_cols), BF16)] * len(weights)
        return pl.pallas_call(
            functools.partial(share_kernel, flips, half_lines),
            out_shape=tuple(out_shape),
            in_specs=[FREE] + [FREE] * len(weights),
            out_specs=(WHOLE,) * len(out_shape),
            scratch_shapes=[pltpu.SemaphoreType.DMA((2 + len(flips) * half_lines,))],
            compiler_params=pltpu.CompilerParams(vmem_limit_bytes=56 * 1024 * 1024),
        )(image_feats, *weights)

    share_x, share_y, key_own = shares(((1, 0), (0, 1)), key_weight)
    share_both, value_own = shares(((1, 1),), value_weight)
    q_mine, q_got = take_y(queries, q_half, y), over_y("q", take_y(queries, q_half, 1 - y))
    low_y = y == 0
    q_rows = jnp.concatenate([jnp.where(low_y, q_mine, q_got), jnp.where(low_y, q_got, q_mine)], 0)
    if fast:
        def devices(route):
            pairs = []
            for l in range(lines):
                for yy in range(2):
                    for c in range(cores):
                        to_l, to_y, to_c = route(l, yy, c)
                        pairs.append(((2 * l + yy) * cores + c, (2 * to_l + to_y) * cores + to_c))
            return pairs

        def to_head(name, tile):
            tiles = []
            for r in range(2):
                with jax.named_scope(name + "_head"):
                    tiles.append(
                        lax.ppermute(
                            tile, ("blk", "heads"), devices(lambda l, yy, c: (2 * c + yy, (l % 2) ^ r, l // 2))
                        )
                    )
            return tiles + [over_core(name + "_tile", t) for t in tiles]

        k1, km = along("wk", key_own, 1), along("wk", key_own, 3, middle)
        img_y, img_x = over_y("image", share_y), over_x("image", share_x)
        kb, ka = along("wk_across", k1, 3, middle), along("wk_out", km, 1, middle)
        kb, ka, img_y, img_x, share_both, value_own, q_rows = hold(kb, ka, img_y, img_x, share_both, value_own, q_rows)
        img_both = over_both("image", share_both)
        ke = along("wk_end", kb, 1, middle)
        v1, vm = along("wv", value_own, 1), along("wv", value_own, 3, middle)
        core_y, core_x = over_core("image", img_y), over_core("image", img_x)
        v1, vm, ke, img_both, core_y, core_x = hold(v1, vm, ke, img_both, core_y, core_x)
        q_1 = along("q", q_rows, 1)
        core_both = over_core("image", img_both)
        vb, va = along("wv_across", v1, 3, middle), along("wv_out", vm, 1, middle)
        pass
        key_refs, value_refs = [key_own, k1, kb, ka, km, ke], [value_own, v1, vb, va, vm]
        pair = lambda i, o: ((i, 0), (o, 0))
        sources = (pair(0, 0), pair(1, 1), pair(2, 3), pair(4, 5))
    else:
        q_pieces = [q_rows if d == 0 else along("q", q_rows, d) for d in range(lines)]
        img_y, img_x, img_both = over_y("image", share_y), over_x("image", share_x), over_both("image", share_both)
        core_y, core_x, core_both = (over_core("image", i) for i in (img_y, img_x, img_both))
        key_refs = [key_own] + [along("wk", key_own, d) for d in range(1, lines)]
        value_refs = [value_own] + [along("wv", value_own, d) for d in range(1, lines)]
        sources = tuple(((d, 0), (d, 0)) for d in range(lines))
    pieces = [img_y, core_y, img_x, core_x, img_both, core_both]
    slots = slot_image.astype(F32).reshape(tok // HD, HD)
    extra = 8 * (-(-(tok // HD) // 8))

    idx = jnp.stack([par, core, y, ((line == 1) | (line == 2)).astype(jnp.int32)] + [line ^ d for d in range(lines)])
    macs = 4 * tok * half * kv_cols

    def project(weights, extra, kind):
        out = lambda rows, dtype: jax.ShapeDtypeStruct((rows, mine_cols), dtype)
        return pl.pallas_call(
            functools.partial(project_kernel, sources, extra),
            out_shape=(out(2 * tok, F32), out(2 * tok + extra, kind), out(2 * tok, kind), out(2 * tok, kind)),
            in_specs=[scalars, WHOLE] + [FREE] * (7 + len(weights)),
            out_specs=(WHOLE,) * 4,
            scratch_shapes=[
                pltpu.VMEM((lines, 4 * tok, half), BF16),
                pltpu.VMEM((lines, half, kv_cols), BF16),
                pltpu.VMEM((4 * tok, kv_cols), F32),
                pltpu.SemaphoreType.DMA((lines, 5)),
            ],
            compiler_params=BIG,
            cost_estimate=pl.CostEstimate(
                flops=2 * macs * lines, bytes_accessed=macs * lines // 32, transcendentals=0
            ),
        )(idx, slots, image_feats, *pieces, *weights)

    rows = 2 * text_rows
    keep, to_y, to_x, to_both = project(key_refs, extra, F32)
    if fast:
        vb, keep, q_1 = hold(vb, keep, q_1)
        q_near = jnp.concatenate([q_rows, q_1], 0)
        q_far = along("q", q_near, 2)
    key_parts = [over_y("key", to_y), over_x("key", to_x), over_both("key", to_both)]
    if fast:
        value_refs.append(along("wv_end", vb, 1, middle))
    slot_rows = 2 * tok // HD
    packed = pl.pallas_call(
        key_kernel,
        out_shape=jax.ShapeDtypeStruct((2 * tok + slot_rows + (-slot_rows % 16), mine_cols), BF16),
        in_specs=[WHOLE] * 6,
        out_specs=WHOLE,
        compiler_params=PARAMS,
    )(keep, *key_parts, key_gain.reshape(1, HD), slots)

    keep, to_y, to_x, to_both = project(value_refs, 0, BF16)
    if fast:
        to_y, to_x, to_both, q_far = hold(to_y, to_x, to_both, q_far)
        q_pieces = [q_near, q_far]
    value_parts = [over_y("value", to_y), over_x("value", to_x), over_both("value", to_both)]
    limits = text_image.astype(F32).reshape(lines, rows)
    limits = jnp.concatenate([lax.dynamic_slice_in_dim(limits, line ^ d, 1, 0) for d in range(lines)], 0)
    limits = limits.reshape(lines * rows, 1)
    all_rows = lines * rows * per_kv
    expo, figures = pl.pallas_call(
        functools.partial(score_kernel, lines, per_kv),
        out_shape=(
            jax.ShapeDtypeStruct((all_rows, 2 * tok), BF16),
            jax.ShapeDtypeStruct((lines * rows, HD), BF16),
        ),
        in_specs=[WHOLE] * (2 + len(q_pieces)),
        out_specs=(WHOLE, WHOLE),
        scratch_shapes=[pltpu.VMEM((per_kv * rows, HD), BF16)],
        compiler_params=PARAMS,
    )(limits, packed, *q_pieces)
    sums = pl.pallas_call(
        functools.partial(value_kernel, lines, per_kv),
        out_shape=(jax.ShapeDtypeStruct((rows, q_half + HD), BF16),) * lines,
        in_specs=[WHOLE] * 6,
        out_specs=(WHOLE,) * lines,
        compiler_params=PARAMS,
    )(expo, figures, keep, *value_parts)
    sums = [sums[0]] + [along("sums", sums[d], d) for d in range(1, lines)]
    attn = pl.pallas_call(
        functools.partial(combine_kernel, lines, per_kv),
        out_shape=jax.ShapeDtypeStruct((rows, q_half), BF16),
        in_specs=[WHOLE] * lines,
        out_specs=WHOLE,
        compiler_params=PARAMS,
    )(*sums)
    mine = [attn if d == 0 else along("attn", attn, d) for d in range(lines)]
    where = [(line ^ d, y) for d in range(lines)] + [(line ^ d, 1 - y) for d in range(lines)]
    other = [over_y(f"attn{d}", m) for d, m in enumerate(mine)]

    out_rows = lines * rows
    out_cols = out_weight.shape[1]
    keep, send = pl.pallas_call(
        functools.partial(proj_kernel, 2 * lines),
        out_shape=(
            jax.ShapeDtypeStruct((out_rows // 2, out_cols), F32),
            jax.ShapeDtypeStruct((out_rows // 2, out_cols), BF16),
        ),
        in_specs=[scalars] + [WHOLE] * (2 * lines) + [FREE],
        out_specs=(WHOLE, WHOLE),
        scratch_shapes=[
            pltpu.VMEM((out_rows, 2 * q_half), BF16),
            pltpu.VMEM((out_rows, out_cols), F32),
            pltpu.VMEM((4, q_half // 2, out_cols), BF16),
            pltpu.SemaphoreType.DMA((4,)),
        ],
        compiler_params=BIG,
    )(jnp.stack([core] + [i for pair in where for i in pair]), *mine, *other, out_weight)
    head_total = keep + over_core("proj", send).astype(F32)
    return (text_hidden.astype(F32) + jnp.tanh(attn_gate[0]) * head_total).astype(BF16)


def solution(mesh):
    placed = (
        P(("groups", "blk"), None),
        P(("groups", "blk")),
        P("blk", "heads"),
        P("blk", "heads"),
        P(),
        P(("groups", "blk"), "heads"),
        P("groups"),
        P(("groups", "heads"), "blk"),
        P("heads", "blk"),
        P(),
    )
    return jax.shard_map(
        body, mesh=mesh, in_specs=placed, out_specs=P(("groups", "heads"), "blk"), check_vma=False
    )
```

```python
import functools
import math

import jax
import jax.numpy as jnp
from jax import lax
from jax.experimental import pallas as pl
from jax.experimental.pallas import tpu as pltpu
from jax.sharding import PartitionSpec as P

HD = 128
F32 = jnp.float32
BF16 = jnp.bfloat16
VMEM_BYTES = 20 * 1024 * 1024
PARAMS = pltpu.CompilerParams(vmem_limit_bytes=VMEM_BYTES)
BIG = pltpu.CompilerParams(vmem_limit_bytes=52 * 1024 * 1024)
WHOLE = pl.BlockSpec(memory_space=pltpu.VMEM)
FREE = pl.BlockSpec(memory_space=pltpu.HBM)


def dot(a, b):
    return jnp.dot(a, b, preferred_element_type=F32)


def dot_nt(a, b):
    return lax.dot_general(a, b, (((1,), (1,)), ((), ())), preferred_element_type=F32)


def share_kernel(flips, half_lines, image, *refs):
    par, core, y = lax.axis_index("groups") % 2, lax.axis_index("heads"), lax.axis_index("blk") % 2
    n = len(flips)
    n_weights = (len(refs) - n - 1) // 2
    weights, outs, sems = refs[:n_weights], refs[n_weights:-1], refs[-1]
    copies = []
    for weight, own in zip(weights, outs[n:]):
        half = own.shape[0]
        copies.append((weight.at[pl.ds(pl.multiple_of(par * half, half), half), :], own))
    for (flip_x, flip_y), out in zip(flips, outs):
        half = out.shape[1] // half_lines
        to_par = 1 - par if flip_x else par
        to_y = 1 - y if flip_y else y
        for l in range(half_lines):
            at = pl.multiple_of(((2 * (core * half_lines + l) + to_y) * 2 + to_par) * half, half)
            copies.append((image.at[:, pl.ds(at, half)], out.at[:, pl.ds(l * half, half)]))
    copies = [pltpu.make_async_copy(src, dst, sems.at[i]) for i, (src, dst) in enumerate(copies)]
    for c in copies:
        c.start()
    for c in copies:
        c.wait()


def load_shards(first, sources, idx_ref, image, got, weights, x_ref, w_ref, sems):
    par, core, y, inner = idx_ref[0], idx_ref[1], idx_ref[2], idx_ref[3]
    rows = image.shape[0]
    half = x_ref.shape[2]
    half_lines = got[0].shape[1] // half
    cols = weights[0].shape[1]

    def copy(src, dst, k, i):
        return pltpu.make_async_copy(src, dst, sems.at[k, i])

    waits = []
    for k, projections in enumerate(sources):
        line = idx_ref[4 + first + k]
        own_at = pl.multiple_of(((2 * line + y) * 2 + par) * half, half)
        here = line // half_lines == core
        got_at = pl.multiple_of(lax.rem(line, half_lines) * half, half)
        own = copy(image.at[:, pl.ds(own_at, half)], x_ref.at[k, pl.ds(0, rows), :], k, 0)
        own.start()

        def from_core(which, k=k, got_at=got_at):
            return [
                copy(
                    got[2 * i + which].at[:, pl.ds(got_at, half)],
                    x_ref.at[k, pl.ds((i + 1) * rows, rows), :],
                    k,
                    1 + i,
                )
                for i in range(3)
            ]

        mine = from_core(0)

        @pl.when(here)
        def _(mine=mine):
            for c in mine:
                c.start()

        @pl.when(jnp.logical_not(here))
        def _(from_core=from_core):
            for c in from_core(1):
                c.start()

        waits.append([own] + mine)
        for p, (in_src, out_src) in enumerate(projections):

            def from_weight(src, k=k, p=p):
                return copy(
                    weights[src[0]].at[pl.ds(src[1], half), :], w_ref.at[k, :, pl.ds(p * cols, cols)], k, 4 + p
                )

            weight = from_weight(in_src)
            if in_src == out_src:
                weight.start()
            else:

                @pl.when(inner > 0)
                def _(weight=weight):
                    weight.start()

                @pl.when(inner <= 0)
                def _(from_weight=from_weight, out_src=out_src):
                    from_weight(out_src).start()

            waits[-1].append(weight)
    return waits


def project_kernel(sources, extra, idx_ref, slots, image, *refs):
    got, weights = refs[:6], refs[6:-8]
    (keep, to_y, to_x, to_both), (x_ref, w_ref, acc_ref, sems) = refs[-8:-4], refs[-4:]
    y = idx_ref[2]
    rows = image.shape[0]
    cols = keep.shape[1]
    kind = to_y.dtype
    waits = load_shards(0, tuple((s,) for s in sources), idx_ref, image, got, weights, x_ref, w_ref, sems)
    for k, copies in enumerate(waits):
        for c in copies:
            c.wait()
        part = dot(x_ref[k], w_ref[k])
        if k == 0:
            acc_ref[...] = part
        elif k < len(waits) - 1:
            acc_ref[...] += part
    total = acc_ref[...] + part
    low = y == 0
    mine = jnp.where(low, total[:, :cols], total[:, cols:])
    other = jnp.where(low, total[:, cols:], total[:, :cols]).astype(kind)
    keep[...] = mine[: 2 * rows]
    to_y[:rows, :] = other[rows : 2 * rows]
    to_y[rows : 2 * rows, :] = other[:rows]
    to_x[...] = mine[2 * rows :].astype(kind)
    to_both[:rows, :] = other[3 * rows :]
    to_both[rows:, :] = other[2 * rows : 3 * rows]
    if extra:
        n = slots.shape[0]
        to_y[2 * rows : 2 * rows + n, :HD] = slots[...]
        to_y[2 * rows + n :, :] = jnp.zeros((extra - n, cols), kind)
        if cols > HD:
            to_y[2 * rows : 2 * rows + n, HD:] = jnp.zeros((n, cols - HD), kind)


def key_kernel(keep, got_y, got_x, got_both, gain, slots, out):
    rows = keep.shape[0]
    n = slots.shape[0]
    raw = (keep[...] + got_y[:rows, :]) + (got_x[...] + got_both[...])
    for c in range(0, raw.shape[1], HD):
        part = raw[:, c : c + HD]
        scale = lax.rsqrt(jnp.mean(part * part, axis=-1, keepdims=True) + 1e-05)
        out[:rows, c : c + HD] = (part * scale * gain[...]).astype(BF16)
    pad = jnp.zeros((out.shape[0] - rows - 2 * n, HD), F32)
    out[rows:, :HD] = jnp.concatenate([slots[...], got_y[rows : rows + n, :HD], pad], 0).astype(BF16)


def score_kernel(n, heads, limit_ref, keys_ref, *refs):
    *queries, expo_ref, figures_ref, q_ref = refs
    rows = limit_ref.shape[0] // n
    each = n // len(queries)
    tokens = expo_ref.shape[1]
    scale = 1.0 / math.sqrt(HD)
    slots = keys_ref[tokens : tokens + 16 * (-(-tokens // HD) // 16 + (-(-tokens // HD) % 16 > 0)), :].astype(F32)
    lane = lax.broadcasted_iota(jnp.int32, (rows, HD), 1)
    for i in range(n):
        limit = limit_ref[i * rows : (i + 1) * rows, :]
        seen = []
        for c in range(tokens // HD):
            slot = slots[c : c + 1, :]
            seen.append(jnp.where((slot >= 0.0) & (slot <= limit), 1.0, 0.0))
        seen = jnp.concatenate(seen, 1)
        for j in range(heads):
            at = i % each * rows
            q_ref[j * rows : (j + 1) * rows, :] = queries[i // each][at : at + rows, j * HD : (j + 1) * HD]
        s = dot_nt(q_ref[...], keys_ref[:tokens, :]) * scale
        s = jnp.where(seen[None] > 0.5, s.reshape(heads, rows, tokens), -1e30).reshape(heads * rows, tokens)
        top = jnp.max(s, axis=1, keepdims=True).astype(BF16).astype(F32)
        e = jnp.where(s > -1e29, jnp.exp(s - top), 0.0)
        total = jnp.sum(e, axis=1, keepdims=True)
        expo_ref[i * heads * rows : (i + 1) * heads * rows, :] = e.astype(BF16)
        high = total.astype(BF16).astype(F32)
        figures = jnp.zeros((rows, HD), F32)
        for j in range(heads):
            part = slice(j * rows, (j + 1) * rows)
            figures = jnp.where(lane == j, top[part], figures)
            figures = jnp.where(lane == heads + j, high[part], figures)
            figures = jnp.where(lane == 2 * heads + j, total[part] - high[part], figures)
        figures_ref[i * rows : (i + 1) * rows, :] = figures.astype(BF16)


def value_kernel(n, heads, expo_ref, figures_ref, keep, got_y, got_x, got_both, *outs):
    rows = figures_ref.shape[0] // n
    values = ((keep[...] + got_y[...].astype(F32)) + (got_x[...].astype(F32) + got_both[...].astype(F32))).astype(BF16)
    for i in range(n):
        acc = dot(expo_ref[i * heads * rows : (i + 1) * heads * rows, :], values).astype(BF16)
        for j in range(heads):
            outs[i][:, j * HD : (j + 1) * HD] = acc[j * rows : (j + 1) * rows, :]
        outs[i][:, heads * HD :] = figures_ref[i * rows : (i + 1) * rows, :]


def combine_kernel(n, heads, *refs):
    parts, out_ref = refs[:n], refs[n]
    rows = out_ref.shape[0]
    lane = lax.broadcasted_iota(jnp.int32, (rows, HD), 1)
    figures = [part[:, heads * HD :].astype(F32) for part in parts]

    def column(figure, at):
        return jnp.sum(jnp.where(lane == at, figure, 0.0), axis=1, keepdims=True)

    for j in range(heads):
        tops = [column(f, j) for f in figures]
        top = functools.reduce(jnp.maximum, tops)
        total = jnp.zeros((rows, 1), F32)
        acc = jnp.zeros((rows, HD), F32)
        for part, figure, own_top in zip(parts, figures, tops):
            weight = jnp.exp(own_top - top)
            total = total + weight * (column(figure, heads + j) + column(figure, 2 * heads + j))
            acc = acc + weight * part[:, j * HD : (j + 1) * HD].astype(F32)
        out_ref[:, j * HD : (j + 1) * HD] = (acc / total).astype(BF16)


def proj_kernel(n, idx_ref, *refs):
    pieces = refs[:n]
    far_ref, keep_ref, send_ref, a_ref, p_ref, w_ref, sems = refs[n:]
    rows, width = pieces[0].shape
    steps, depth = w_ref.shape[:2]
    copies = [
        pltpu.make_async_copy(far_ref.at[pl.ds(i * depth, depth), :], w_ref.at[i], sems.at[i]) for i in range(steps)
    ]
    for c in copies:
        c.start()
    for k in range(n):
        at_row = pl.multiple_of(idx_ref[1 + 2 * k] * rows, rows)
        at_col = pl.multiple_of(idx_ref[2 + 2 * k] * width, width)
        a_ref[pl.ds(at_row, rows), pl.ds(at_col, width)] = pieces[k][...]
    for i, c in enumerate(copies):
        c.wait()
        part = dot(a_ref[:, i * depth : (i + 1) * depth], w_ref[i])
        if i == 0:
            p_ref[...] = part
        else:
            p_ref[...] += part
    size = keep_ref.shape[0]
    core = idx_ref[0]
    keep_ref[...] = p_ref[pl.ds(pl.multiple_of(core * size, size), size), :]
    send_ref[...] = p_ref[pl.ds(pl.multiple_of((1 - core) * size, size), size), :].astype(BF16)


def body(
    image_feats,
    slot_image,
    key_weight,
    value_weight,
    key_gain,
    queries,
    text_image,
    text_hidden,
    out_weight,
    attn_gate,
):
    groups, nblk, cores = (lax.axis_size(a) for a in ("groups", "blk", "heads"))
    lines = nblk // 2
    tok = image_feats.shape[0]
    depth = key_weight.shape[0]
    kv_cols = key_weight.shape[1]
    mine_cols = kv_cols // 2
    text_rows = queries.shape[0]
    q_half = queries.shape[1] // 2
    per_kv = q_half // mine_cols
    grp, blk, core = (lax.axis_index(a) for a in ("groups", "blk", "heads"))
    par = grp % 2
    y = blk % 2
    line = blk // 2

    swap_y = [(b, b ^ 1) for b in range(nblk)]
    swap_core = [(c, c ^ 1) for c in range(cores)]
    half = depth // 2
    fast = lines == 4 and cores == 2 and kv_cols == 2 * HD

    def along(name, array, d, ok=lambda l: True):
        with jax.named_scope(f"{name}_z{d}"):
            return lax.ppermute(array, "blk", [(b, b ^ (2 * d)) for b in range(nblk) if ok(b // 2)])

    def over_y(name, array):
        with jax.named_scope(name + "_y"):
            return lax.ppermute(array, "blk", swap_y)

    def over_core(name, array):
        with jax.named_scope(name + "_core"):
            return lax.ppermute(array, "heads", swap_core)

    def over_x(name, array):
        with jax.named_scope(name + "_x"):
            return lax.ppermute(array, "groups", [(g, g ^ 1) for g in range(groups)])

    def over_both(name, array):
        pairs = [(g * nblk + b, (g ^ 1) * nblk + (b ^ 1)) for g in range(groups) for b in range(nblk)]
        with jax.named_scope(name + "_xy"):
            return lax.ppermute(array, ("groups", "blk"), pairs)

    def hold(*arrays):
        return lax.optimization_barrier(arrays)

    def take_y(array, size, which):
        return lax.dynamic_slice_in_dim(array, which * size, size, 1)

    def middle(l):
        return l in (1, 2)

    half_lines = lines // 2

    def share(to_x, to_y):
        return jnp.concatenate(
            [
                lax.dynamic_slice_in_dim(
                    image_feats, ((2 * (core * half_lines + l) + to_y) * 2 + to_x) * half, half, 1
                )
                for l in range(half_lines)
            ],
            1,
        )

    half_lines = lines // 2
    scalars = pl.BlockSpec(memory_space=pltpu.SMEM)
    share = jax.ShapeDtypeStruct((tok, half_lines * half), BF16)

    def shares(flips, *weights):
        out_shape = [share] * len(flips) + [jax.ShapeDtypeStruct((half, kv_cols), BF16)] * len(weights)
        return pl.pallas_call(
            functools.partial(share_kernel, flips, half_lines),
            out_shape=tuple(out_shape),
            in_specs=[FREE] + [FREE] * len(weights),
            out_specs=(WHOLE,) * len(out_shape),
            scratch_shapes=[pltpu.SemaphoreType.DMA((2 + len(flips) * half_lines,))],
            compiler_params=pltpu.CompilerParams(vmem_limit_bytes=56 * 1024 * 1024),
        )(image_feats, *weights)

    share_x, share_y, key_own = shares(((1, 0), (0, 1)), key_weight)
    share_both, value_own = shares(((1, 1),), value_weight)
    q_mine, q_got = take_y(queries, q_half, y), over_y("q", take_y(queries, q_half, 1 - y))
    low_y = y == 0
    q_rows = jnp.concatenate([jnp.where(low_y, q_mine, q_got), jnp.where(low_y, q_got, q_mine)], 0)
    if fast:
        def devices(route):
            pairs = []
            for l in range(lines):
                for yy in range(2):
                    for c in range(cores):
                        to_l, to_y, to_c = route(l, yy, c)
                        pairs.append(((2 * l + yy) * cores + c, (2 * to_l + to_y) * cores + to_c))
            return pairs

        def to_head(name, tile):
            tiles = []
            for r in range(2):
                with jax.named_scope(name + "_head"):
                    tiles.append(
                        lax.ppermute(
                            tile, ("blk", "heads"), devices(lambda l, yy, c: (2 * c + yy, (l % 2) ^ r, l // 2))
                        )
                    )
            return tiles + [over_core(name + "_tile", t) for t in tiles]

        k1, km = along("wk", key_own, 1), along("wk", key_own, 3, middle)
        img_y, img_x = over_y("image", share_y), over_x("image", share_x)
        kb, ka = along("wk_across", k1, 3, middle), along("wk_out", km, 1, middle)
        kb, ka, img_y, img_x, share_both, value_own, q_rows = hold(kb, ka, img_y, img_x, share_both, value_own, q_rows)
        img_both = over_both("image", share_both)
        ke = along("wk_end", kb, 1, middle)
        v1, vm = along("wv", value_own, 1), along("wv", value_own, 3, middle)
        core_y, core_x = over_core("image", img_y), over_core("image", img_x)
        v1, vm, ke, img_both, core_y, core_x = hold(v1, vm, ke, img_both, core_y, core_x)
        q_1 = along("q", q_rows, 1)
        core_both = over_core("image", img_both)
        vb, va = along("wv_across", v1, 3, middle), along("wv_out", vm, 1, middle)
        pass
        key_refs, value_refs = [key_own, k1, kb, ka, km, ke], [value_own, v1, vb, va, vm]
        pair = lambda i, o: ((i, 0), (o, 0))
        sources = (pair(0, 0), pair(1, 1), pair(2, 3), pair(4, 5))
    else:
        q_pieces = [q_rows if d == 0 else along("q", q_rows, d) for d in range(lines)]
        img_y, img_x, img_both = over_y("image", share_y), over_x("image", share_x), over_both("image", share_both)
        core_y, core_x, core_both = (over_core("image", i) for i in (img_y, img_x, img_both))
        key_refs = [key_own] + [along("wk", key_own, d) for d in range(1, lines)]
        value_refs = [value_own] + [along("wv", value_own, d) for d in range(1, lines)]
        sources = tuple(((d, 0), (d, 0)) for d in range(lines))
    pieces = [img_y, core_y, img_x, core_x, img_both, core_both]
    slots = slot_image.astype(F32).reshape(tok // HD, HD)
    extra = 8 * (-(-(tok // HD) // 8))

    idx = jnp.stack([par, core, y, ((line == 1) | (line == 2)).astype(jnp.int32)] + [line ^ d for d in range(lines)])
    macs = 4 * tok * half * kv_cols

    def project(weights, extra, kind):
        out = lambda rows, dtype: jax.ShapeDtypeStruct((rows, mine_cols), dtype)
        return pl.pallas_call(
            functools.partial(project_kernel, sources, extra),
            out_shape=(out(2 * tok, F32), out(2 * tok + extra, kind), out(2 * tok, kind), out(2 * tok, kind)),
            in_specs=[scalars, WHOLE] + [FREE] * (7 + len(weights)),
            out_specs=(WHOLE,) * 4,
            scratch_shapes=[
                pltpu.VMEM((lines, 4 * tok, half), BF16),
                pltpu.VMEM((lines, half, kv_cols), BF16),
                pltpu.VMEM((4 * tok, kv_cols), F32),
                pltpu.SemaphoreType.DMA((lines, 5)),
            ],
            compiler_params=BIG,
            cost_estimate=pl.CostEstimate(
                flops=2 * macs * lines, bytes_accessed=macs * lines // 32, transcendentals=0
            ),
        )(idx, slots, image_feats, *pieces, *weights)

    rows = 2 * text_rows
    keep, to_y, to_x, to_both = project(key_refs, extra, F32)
    if fast:
        vb, keep, q_1 = hold(vb, keep, q_1)
        q_near = jnp.concatenate([q_rows, q_1], 0)
        q_far = along("q", q_near, 2)
    key_parts = [over_y("key", to_y), over_x("key", to_x), over_both("key", to_both)]
    if fast:
        value_refs.append(along("wv_end", vb, 1, middle))
    slot_rows = 2 * tok // HD
    packed = pl.pallas_call(
        key_kernel,
        out_shape=jax.ShapeDtypeStruct((2 * tok + slot_rows + (-slot_rows % 16), mine_cols), BF16),
        in_specs=[WHOLE] * 6,
        out_specs=WHOLE,
        compiler_params=PARAMS,
    )(keep, *key_parts, key_gain.reshape(1, HD), slots)

    keep, to_y, to_x, to_both = project(value_refs, 0, BF16)
    if fast:
        to_y, to_x, to_both, q_far = hold(to_y, to_x, to_both, q_far)
        q_pieces = [q_near, q_far]
    value_parts = [over_y("value", to_y), over_x("value", to_x), over_both("value", to_both)]
    limits = text_image.astype(F32).reshape(lines, rows)
    limits = jnp.concatenate([lax.dynamic_slice_in_dim(limits, line ^ d, 1, 0) for d in range(lines)], 0)
    limits = limits.reshape(lines * rows, 1)
    all_rows = lines * rows * per_kv
    expo, figures = pl.pallas_call(
        functools.partial(score_kernel, lines, per_kv),
        out_shape=(
            jax.ShapeDtypeStruct((all_rows, 2 * tok), BF16),
            jax.ShapeDtypeStruct((lines * rows, HD), BF16),
        ),
        in_specs=[WHOLE] * (2 + len(q_pieces)),
        out_specs=(WHOLE, WHOLE),
        scratch_shapes=[pltpu.VMEM((per_kv * rows, HD), BF16)],
        compiler_params=PARAMS,
    )(limits, packed, *q_pieces)
    sums = pl.pallas_call(
        functools.partial(value_kernel, lines, per_kv),
        out_shape=(jax.ShapeDtypeStruct((rows, q_half + HD), BF16),) * lines,
        in_specs=[WHOLE] * 6,
        out_specs=(WHOLE,) * lines,
        compiler_params=PARAMS,
    )(expo, figures, keep, *value_parts)
    far_first = sorted(range(1, lines), key=lambda d: (d < 2, d))
    moved = {d: along("sums", sums[d], d) for d in far_first}
    sums = [sums[0]] + [moved[d] for d in range(1, lines)]
    attn = pl.pallas_call(
        functools.partial(combine_kernel, lines, per_kv),
        out_shape=jax.ShapeDtypeStruct((rows, q_half), BF16),
        in_specs=[WHOLE] * lines,
        out_specs=WHOLE,
        compiler_params=PARAMS,
    )(sums[0], *(sums[d] for d in far_first))
    moved = {d: along("attn", attn, d) for d in far_first}
    order = [0] + far_first
    mine = [attn if d == 0 else moved[d] for d in order]
    where = [(line ^ d, y) for d in order] + [(line ^ d, 1 - y) for d in order]
    other = [over_y(f"attn{d}", m) for d, m in enumerate(mine)]

    out_rows = lines * rows
    out_cols = out_weight.shape[1]
    keep, send = pl.pallas_call(
        functools.partial(proj_kernel, 2 * lines),
        out_shape=(
            jax.ShapeDtypeStruct((out_rows // 2, out_cols), F32),
            jax.ShapeDtypeStruct((out_rows // 2, out_cols), BF16),
        ),
        in_specs=[scalars] + [WHOLE] * (2 * lines) + [FREE],
        out_specs=(WHOLE, WHOLE),
        scratch_shapes=[
            pltpu.VMEM((out_rows, 2 * q_half), BF16),
            pltpu.VMEM((out_rows, out_cols), F32),
            pltpu.VMEM((4, q_half // 2, out_cols), BF16),
            pltpu.SemaphoreType.DMA((4,)),
        ],
        compiler_params=BIG,
    )(jnp.stack([core] + [i for pair in where for i in pair]), *mine, *other, out_weight)
    head_total = keep + over_core("proj", send).astype(F32)
    return (text_hidden.astype(F32) + jnp.tanh(attn_gate[0]) * head_total).astype(BF16)


def solution(mesh):
    placed = (
        P(("groups", "blk"), None),
        P(("groups", "blk")),
        P("blk", "heads"),
        P("blk", "heads"),
        P(),
        P(("groups", "blk"), "heads"),
        P("groups"),
        P(("groups", "heads"), "blk"),
        P("heads", "blk"),
        P(),
    )
    return jax.shard_map(
        body, mesh=mesh, in_specs=placed, out_specs=P(("groups", "heads"), "blk"), check_vma=False
    )
```
